32 devices in a mesh: dp: 8 (over z, y), fsdp: 4 (over x, core).
Axes of the slice: x: 2, y: 2, z: 4, core: 2. Of those that a mesh axis runs over, the one named last changes fastest.
Arguments:
- tokens: bfloat16 [49152, 768], P(('dp', 'fsdp')), may hold values from -6 to 6
- cotangent: bfloat16 [49152, 768], P(('dp', 'fsdp')), may hold values from -6 to 6
- bucket: int32 [32], P(('dp', 'fsdp')), may hold values from 0 to 2, as said below
- key_lengths: int32 [32, 3], P(('dp', 'fsdp')), may hold values from 0 to 1536, as said below
- query_weight: bfloat16 [768, 768], P('fsdp'), may hold values from -0.21875 to 0.21875
- key_weight: bfloat16 [768, 768], P('fsdp'), may hold values from -0.21875 to 0.21875
- value_weight: bfloat16 [768, 768], P('fsdp'), may hold values from -0.21875 to 0.21875
- output_weight: bfloat16 [768, 768], P('fsdp'), may hold values from -4 to 4
- up_weight: bfloat16 [768, 3072], P('fsdp'), may hold values from -0.21875 to 0.21875
- down_weight: bfloat16 [3072, 768], P('fsdp'), may hold values from -0.109375 to 0.109375
- query_bias: bfloat16 [768], P('fsdp'), may hold values from -3 to 3
- key_bias: bfloat16 [768], P('fsdp'), may hold values from -3 to 3
- value_bias: bfloat16 [768], P('fsdp'), may hold values from -3 to 3
- output_bias: bfloat16 [768], P('fsdp'), may hold values from -2 to 2
- up_bias: bfloat16 [3072], P('fsdp'), may hold values from -3 to 3
- down_bias: bfloat16 [768], P('fsdp'), may hold values from -2 to 2
- first_gain: bfloat16 [768], P('fsdp'), may hold values from 0.5 to 1.5
- first_shift: bfloat16 [768], P('fsdp'), may hold values from -2 to 2
- second_gain: bfloat16 [768], P('fsdp'), may hold values from 0.5 to 1.5
- second_shift: bfloat16 [768], P('fsdp'), may hold values from -2 to 2
Outputs:
- layer_output: bfloat16 [49152, 768], P(('dp', 'fsdp'))
- token_grad: bfloat16 [49152, 768], P(('dp', 'fsdp'))
- query_weight_grad: float32 [768, 768], P('fsdp')
- key_weight_grad: float32 [768, 768], P('fsdp')
- value_weight_grad: float32 [768, 768], P('fsdp')
- output_weight_grad: float32 [768, 768], P('fsdp')
- up_weight_grad: float32 [768, 3072], P('fsdp')
- down_weight_grad: float32 [3072, 768], P('fsdp')
- query_bias_grad: float32 [768], P('fsdp')
- key_bias_grad: float32 [768], P('fsdp')
- value_bias_grad: float32 [768], P('fsdp')
- output_bias_grad: float32 [768], P('fsdp')
- up_bias_grad: float32 [3072], P('fsdp')
- down_bias_grad: float32 [768], P('fsdp')
- first_gain_grad: float32 [768], P('fsdp')
- first_shift_grad: float32 [768], P('fsdp')
- second_gain_grad: float32 [768], P('fsdp')
- second_shift_grad: float32 [768], P('fsdp')
The draws below stay inside these ranges and needn't reach their ends.
Inputs may be any that keep to these rules, and one draw needn't show every extreme that they name: bucket[g] = 0: three sequences of 512 places; 1: one of 1024 then one of 512; 2: one of 1536. Every layout occurs in every draw. `key_lengths`: entry j counts the unpadded tokens at the start of the group's j-th sequence: from half its places (rounded up) to all of them; 0 where the layout has fewer than j + 1 sequences. Places after them are padding, whose keys are masked. In every draw each layout occurs on some group with no padding.
All inputs are finite; a program needn't handle non-finite values.
Results may differ from the reference program's by a relative error of at most 0.015.
Values may be sent and summed in bfloat16 or wider, within the bound.
No kernel may reach another device: no remote copies, remote signals or barrier semaphores. Data moves between devices by JAX's collectives and lax.ppermute only.
A program may use at most 256 MiB of HBM per device.

```python
import jax
import jax.numpy as jnp
from jax import lax

D = 768
HEAD_DIM = 64
FF = 3072
SLOT = 512
TOK_DEV = 1536
SHARDS = 32
TOKENS = 49152


def shared_layouts(key):
    chosen = jax.random.randint(jax.random.fold_in(key, 11), (SHARDS,), 0, 3, dtype=jnp.int32)
    first_three = jax.random.permutation(jax.random.fold_in(key, 12), 3).astype(jnp.int32)
    return chosen.at[:3].set(first_three)


def draw_bucket(key, part):
    layouts = shared_layouts(key)
    return layouts


def draw_key_lengths(key, part):
    layouts = shared_layouts(key)
    key = jax.random.fold_in(key, 5)
    whole_len = jnp.where(layouts == 0, SLOT, jnp.where(layouts == 1, 2 * SLOT, 3 * SLOT))
    middle_len = jnp.where(layouts == 2, 0, SLOT)
    third_len = jnp.where(layouts == 0, SLOT, 0)
    lengths = jnp.stack([whole_len, middle_len, third_len], axis=1).astype(jnp.int32)
    raw_bits = jax.random.randint(key, (SHARDS, 3), 0, 1 << 20, dtype=jnp.int32)
    padding = raw_bits % (lengths // 2 + 1)
    row_index = jnp.arange(SHARDS, dtype=jnp.int32)[:, None]
    padding = jnp.where(row_index < 3, 0, padding)
    return (lengths - padding).astype(jnp.int32)


def levels(own_key, shape, split, smallest, largest):
    def one(dim, parts):
        heights = jax.random.uniform(jax.random.fold_in(jax.random.fold_in(own_key, 6), dim), (parts,), jnp.float32, smallest / len(split), largest / len(split))
        return jnp.repeat(jnp.exp(heights), shape[dim] // parts).reshape((-1,) + (1,) * (len(shape) - dim - 1))

    factor_of = one(*split[0])
    for cut in split[1:]:
        factor_of = factor_of * one(*cut)
    return factor_of


def centred(stream_key, dims, deviation, bound, pieces=(), kind=jnp.bfloat16):
    values = jax.random.normal(stream_key, dims, jnp.float32) * deviation
    if len(pieces) > 0:
        values = levels(stream_key, dims, pieces, -0.22, 0.18) * values
    return jnp.clip(values, min=-bound, max=bound).astype(kind)


def setup_inputs(seed: int = 0) -> dict:
    seeds = jax.random.split(jax.random.key(seed), 21)
    tokens = centred(seeds[0], (TOKENS, D), 1.0, 6.0, ((0, 32),))
    cotangent = centred(seeds[1], (TOKENS, D), 1.0, 6.0, ((0, 32),))
    bucket = draw_bucket(jax.random.fold_in(seeds[20], 71), 0)
    key_lengths = draw_key_lengths(jax.random.fold_in(seeds[20], 71), 0)
    query_weight = centred(seeds[4], (D, D), D ** -0.5, 0.21875, ((0, 4),))
    key_weight = centred(seeds[5], (D, D), D ** -0.5, 0.21875, ((0, 4),))
    value_weight = centred(seeds[6], (D, D), D ** -0.5, 0.21875, ((0, 4),))
    output_weight = centred(seeds[7], (D, D), 2 ** -0.5, 4.0, ((0, 4),))
    up_weight = centred(seeds[8], (D, FF), D ** -0.5, 0.21875, ((0, 4),))
    down_weight = centred(seeds[9], (FF, D), FF ** -0.5, 0.109375, ((0, 4),))
    query_bias = centred(seeds[10], (D,), 0.5, 3.0, ((0, 4),))
    key_bias = centred(seeds[11], (D,), 0.5, 3.0, ((0, 4),))
    value_bias = centred(seeds[12], (D,), 0.5, 3.0, ((0, 4),))
    output_bias = centred(seeds[13], (D,), 0.3, 2.0, ((0, 4),))
    up_bias = centred(seeds[14], (FF,), 0.5, 3.0, ((0, 4),))
    down_bias = centred(seeds[15], (D,), 0.3, 2.0, ((0, 4),))
    first_gain = jnp.clip(1.0 + 0.1 * jax.random.normal(seeds[16], (D,), jnp.float32), 0.5, 1.5).astype(jnp.bfloat16)
    first_shift = centred(seeds[17], (D,), 0.3, 2.0, ((0, 4),))
    second_gain = jnp.clip(1.0 + 0.1 * jax.random.normal(seeds[18], (D,), jnp.float32), 0.5, 1.5).astype(jnp.bfloat16)
    second_shift = centred(seeds[19], (D,), 0.3, 2.0, ((0, 4),))
    return {"tokens": tokens, "cotangent": cotangent, "bucket": bucket, "key_lengths": key_lengths, "query_weight": query_weight, "key_weight": key_weight, "value_weight": value_weight, "output_weight": output_weight, "up_weight": up_weight, "down_weight": down_weight, "query_bias": query_bias, "key_bias": key_bias, "value_bias": value_bias, "output_bias": output_bias, "up_bias": up_bias, "down_bias": down_bias, "first_gain": first_gain, "first_shift": first_shift, "second_gain": second_gain, "second_shift": second_shift}


@jax.custom_vjp
def low(v):
    return lax.optimization_barrier(v.astype(jnp.bfloat16)).astype(jnp.float32)

@jax.custom_vjp
def low_back(v):
    return v

def low_keep(v):
    return (low(v), None)

def low_pass(kept, grad):
    return (grad,)

def back_keep(v):
    return (v, None)

def back_low(kept, grad):
    return (low(grad),)
low.defvjp(low_keep, low_pass)
low_back.defvjp(back_keep, back_low)

def dense_product(left_side, right_side):
    return jnp.dot(left_side, right_side, precision=lax.Precision.HIGHEST, preferred_element_type=jnp.float32)

def layout_tables(bucket_value, lengths_row, row_count, slot_len):
    places = jnp.arange(row_count, dtype=jnp.int32)
    slot_index = places // slot_len
    sequence = jnp.where(bucket_value == 0, slot_index, jnp.where(bucket_value == 1, slot_index // 2, 0))
    starts = jnp.where(bucket_value == 0, slot_index * slot_len, jnp.where(bucket_value == 1, slot_index // 2 * 2 * slot_len, 0))
    offsets = places - starts
    limits = jnp.zeros_like(places)
    for member in range(3):
        limits = limits + jnp.where(sequence == member, lengths_row[member], 0)
    allowed = (sequence[:, None] == sequence[None, :]) & (offsets < limits)[None, :]
    return (allowed, offsets)

def rotary_tables(offsets, head_dim):
    half_dim = head_dim // 2
    exponents = jnp.arange(half_dim, dtype=jnp.float32) * (-2.0 / head_dim)
    inverse = jnp.power(jnp.float32(10000.0), exponents)
    angles = offsets.astype(jnp.float32)[:, None] * inverse[None, :]
    return (jnp.cos(angles)[:, None, :], jnp.sin(angles)[:, None, :])

def rotate(values, cosine, sine_table):
    row_count = values.shape[0]
    half_dim = cosine.shape[-1]
    shaped = values.reshape(row_count, -1, 2, half_dim)
    first_half = shaped[:, :, 0]
    second_half = shaped[:, :, 1]
    turned = jnp.stack([first_half * cosine - second_half * sine_table, second_half * cosine + first_half * sine_table], axis=2)
    return turned.reshape(row_count, -1)

def layer_norm(rows_in, gain_row, shift_row):
    center = rows_in - lax.optimization_barrier(jnp.mean(rows_in, axis=-1, keepdims=True))
    spread = lax.optimization_barrier(jnp.mean(center * center, axis=-1, keepdims=True))
    return center * lax.rsqrt(spread + 1e-05) * gain_row + shift_row

def group_layer(params_in, group_rows, bucket_value, lengths_row):
    query_weight, key_weight, value_weight, output_weight, up_weight, down_weight, query_bias, key_bias, value_bias, output_bias, up_bias, down_bias, first_gain, first_shift, second_gain, second_shift = params_in
    row_count = group_rows.shape[0]
    head_count = D // HEAD_DIM
    allowed, offsets = layout_tables(bucket_value, lengths_row, row_count, SLOT)
    cosine, sine_table = rotary_tables(offsets, HEAD_DIM)
    query_rows = low_back(dense_product(group_rows, query_weight) + query_bias)
    key_rows = low_back(dense_product(group_rows, key_weight) + key_bias)
    value_rows = low(low_back(dense_product(group_rows, value_weight) + value_bias))
    query_rot = low(rotate(query_rows, cosine, sine_table)).reshape(row_count, head_count, HEAD_DIM)
    key_rot = low(rotate(key_rows, cosine, sine_table)).reshape(row_count, head_count, HEAD_DIM)
    scores = low_back(jnp.einsum('qhd,khd->hqk', query_rot, key_rot, precision=lax.Precision.HIGHEST) * 0.125)
    scores = jnp.where(allowed[None], scores, -1e+30)
    row_max = lax.optimization_barrier(jnp.max(scores, axis=-1, keepdims=True))
    exp_scores = jnp.exp(scores - row_max)
    weights_low = low(exp_scores / lax.optimization_barrier(jnp.sum(exp_scores, axis=-1, keepdims=True)))
    mixed_rows = jnp.einsum('hqk,khd->qhd', weights_low, value_rows.reshape(row_count, head_count, HEAD_DIM), precision=lax.Precision.HIGHEST).reshape(row_count, D)
    mixed_rows = low(low_back(mixed_rows))
    attended = low_back(dense_product(mixed_rows, output_weight) + output_bias)
    hidden = layer_norm(group_rows + attended, first_gain, first_shift)
    inner_pre = low_back(dense_product(low(hidden), up_weight) + up_bias)
    activated = low(jax.nn.gelu(inner_pre, approximate=False))
    branch = low_back(dense_product(activated, down_weight) + down_bias)
    return layer_norm(hidden + branch, second_gain, second_shift)

def reference(tokens, cotangent, bucket, key_lengths, query_weight, key_weight, value_weight, output_weight, up_weight, down_weight, query_bias, key_bias, value_bias, output_bias, up_bias, down_bias, first_gain, first_shift, second_gain, second_shift):
    params = tuple((weight_arg.astype(jnp.float32) for weight_arg in (query_weight, key_weight, value_weight, output_weight, up_weight, down_weight, query_bias, key_bias, value_bias, output_bias, up_bias, down_bias, first_gain, first_shift, second_gain, second_shift)))
    inputs = tokens.astype(jnp.float32).reshape(-1, TOK_DEV, D)
    grads_in = cotangent.astype(jnp.float32).reshape(-1, TOK_DEV, D)

    def forward(group_inputs, params_in):

        def one_group(operands):
            return group_layer(params_in, operands[0], operands[1], operands[2])
        return lax.map(jax.checkpoint(one_group), (group_inputs, bucket, key_lengths))
    result, pullback = jax.vjp(forward, inputs, params)
    input_grad, param_grads = pullback(grads_in)
    return (result.reshape(-1, D).astype(jnp.bfloat16), input_grad.reshape(-1, D).astype(jnp.bfloat16), param_grads[0], param_grads[1], param_grads[2], param_grads[3], param_grads[4], param_grads[5], param_grads[6], param_grads[7], param_grads[8], param_grads[9], param_grads[10], param_grads[11], param_grads[12], param_grads[13], param_grads[14], param_grads[15])
```

```python
import functools

import jax
import jax.numpy as jnp
from jax import lax
from jax.experimental import pallas as pl
from jax.experimental.pallas import tpu as pltpu
from jax.sharding import PartitionSpec as P

HEAD_DIM = 64
HALF = 32
SLOT = 512
AUX = 16
NEG = -1e30
LOG2E = 1.4426950408889634
LN2 = 0.6931471805599453
QSCALE = 0.125 * LOG2E
BF = jnp.bfloat16
F32 = jnp.float32
NN = ((1,), (0,))
NT = ((1,), (1,))
TN = ((0,), (0,))
ERFC_P = 0.37
ERFC_C = (
    0.20835304049472436,
    0.2152118908535975,
    0.15105251587527643,
    0.3213824037594925,
    -0.19174412290346565,
    0.4392956874015427,
    -0.14355086909593573,
)
VMEM_LIMIT = 60 << 20


def lasts(us):
    return pl.CostEstimate(flops=us * 1000000000, bytes_accessed=us * 3000000, transcendentals=0)


def dot(a, b, dims=NN):
    return lax.dot_general(a, b, (dims, ((), ())), preferred_element_type=F32)


def params(**kw):
    return pltpu.CompilerParams(vmem_limit_bytes=VMEM_LIMIT, **kw)


def const_spec(shape):
    return pl.BlockSpec(shape, lambda *_: (0,) * len(shape), pipeline_mode=pl.Buffered(1))


def layout_tables(bucket_value, lengths_row, row_count):
    places = jnp.arange(row_count, dtype=jnp.int32)
    slot_index = places // SLOT
    sequence = jnp.where(
        bucket_value == 0, slot_index, jnp.where(bucket_value == 1, slot_index // 2, 0)
    )
    starts = jnp.where(
        bucket_value == 0,
        slot_index * SLOT,
        jnp.where(bucket_value == 1, slot_index // 2 * 2 * SLOT, 0),
    )
    offsets = places - starts
    limits = jnp.zeros_like(places)
    for member in range(3):
        limits = limits + jnp.where(sequence == member, lengths_row[member], 0)
    valid = offsets < limits
    rows = jnp.arange(AUX, dtype=jnp.int32)[:, None]
    same = (rows == sequence[None, :]) & (rows < 3)
    aux_q = jnp.where(same, 1.0, 0.0).astype(BF)
    aux_k = jnp.where(
        rows < 3,
        jnp.where(same & valid[None, :], 0.0, NEG),
        jnp.where(rows < 6, 1.0, 0.0),
    ).astype(BF)
    exponents = jnp.arange(HALF, dtype=F32) * (-2.0 / HEAD_DIM)
    inverse = jnp.power(jnp.float32(10000.0), exponents)
    angles = inverse[:, None] * offsets.astype(F32)[None, :]
    return aux_q, aux_k, jnp.cos(angles), jnp.sin(angles)


def turn(z, cos, sin):
    a, b = z[:HALF], z[HALF:]
    return jnp.concatenate([a * cos - b * sin, b * cos + a * sin], axis=0)


def pack_kernel(cut, wq, wk, wv, one, two):
    depth = wq.shape[1]
    for t, w in enumerate((wq, wk, wv)):
        one[:, t * cut : (t + 1) * cut] = w[:, :cut]
        two[:, t * (depth - cut) : (t + 1) * (depth - cut)] = w[:, cut:]


def pack(wq, wk, wv, cut):
    rows, depth = wq.shape
    sizes = [(rows, 3 * cut), (rows, 3 * (depth - cut))]
    return pl.pallas_call(
        functools.partial(pack_kernel, cut),
        grid=(1,),
        in_specs=[const_spec(wq.shape)] * 3,
        out_specs=[const_spec(z) for z in sizes],
        out_shape=[jax.ShapeDtypeStruct(z, BF) for z in sizes],
        compiler_params=params(),
        cost_estimate=lasts(2),
        name="pack",
    )(wq, wk, wv)


def split_kernel(side, w, here, away):
    half = here.shape[1]
    here[...] = w[:, pl.ds(pl.multiple_of(side[0] * half, half), half)]
    away[...] = w[:, pl.ds(pl.multiple_of((1 - side[0]) * half, half), half)]


def split(side, w):
    rows, wide = w.shape
    size = (rows, wide // 2)
    return pl.pallas_call(
        split_kernel,
        grid_spec=pltpu.PrefetchScalarGridSpec(
            num_scalar_prefetch=1,
            grid=(1,),
            in_specs=[const_spec(w.shape)],
            out_specs=[const_spec(size)] * 2,
        ),
        out_shape=[jax.ShapeDtypeStruct(size, BF)] * 2,
        compiler_params=params(),
        cost_estimate=lasts(2),
        name="split",
    )(side, w)


def attn_fwd_kernel(chunk, count, me, xt, *refs):
    pieces_in, refs = refs[: 3 * count], refs[3 * count :]
    bias, cos, sin, aux_q, aux_k, qt, kt, vt, ot, lse, wq, wk, wv, acc, top = refs
    tokens = xt.shape[1]
    x = xt[...]
    for col, (w, out) in enumerate(((wq, qt), (wk, kt), (wv, vt))):
        for j in range(count):
            piece = pieces_in[col * count + j]
            rows = piece.shape[0]
            w[pl.ds(pl.multiple_of((me[0] ^ j) * rows, rows), rows), :] = piece[...]
        z = dot(w[...], x, TN) + bias[:, col : col + 1]
        if col == 2:
            out[...] = z.astype(BF)
            continue
        for h in range(2):
            r = turn(z[h * HEAD_DIM : (h + 1) * HEAD_DIM], cos[...], sin[...])
            if col == 0:
                r = r * QSCALE
            out[h * HEAD_DIM : (h + 1) * HEAD_DIM, :] = r.astype(BF)
    ones = jnp.ones((AUX, tokens), BF)
    for h in range(2):
        rows = slice(h * HEAD_DIM, (h + 1) * HEAD_DIM)
        q32 = qt[rows, :].astype(F32)
        k32 = kt[rows, :].astype(F32)
        bound = jnp.max(jnp.sum(q32 * q32, axis=0)) * jnp.max(jnp.sum(k32 * k32, axis=0))
        qa = jnp.concatenate([qt[rows, :], aux_q[...]], axis=0)
        ka = jnp.concatenate([kt[rows, :], aux_k[...]], axis=0).T
        va = jnp.concatenate([vt[rows, :], ones], axis=0)
        small = bound < 8100.0

        @pl.when(small)
        def _():
            total = None
            for c in range(tokens // chunk):
                sl = slice(c * chunk, (c + 1) * chunk)
                p = jnp.exp2(dot(ka[sl], qa)).astype(BF)
                part = dot(va[:, sl], p)
                total = part if total is None else total + part
            acc[...] = total
            top[...] = jnp.zeros_like(top)

        @pl.when(jnp.logical_not(small))
        def _():
            total = None
            for c in range(tokens // chunk):
                sl = slice(c * chunk, (c + 1) * chunk)
                s = dot(ka[sl], qa)
                here = jnp.max(s, axis=0, keepdims=True)
                if c == 0:
                    best = here
                    total = dot(va[:, sl], jnp.exp2(s - best).astype(BF))
                else:
                    later = jnp.maximum(best, here)
                    part = dot(va[:, sl], jnp.exp2(s - later).astype(BF))
                    total = total * jnp.exp2(best - later) + part
                    best = later
            acc[...] = total
            top[...] = best

        row_total = acc[HEAD_DIM : HEAD_DIM + 1, :]
        ot[rows, :] = (acc[:HEAD_DIM, :] / row_total).astype(BF)
        lse[0, h : h + 1, :] = top[...] + jnp.log2(row_total)


def attn_fwd(me, first, pairs, xt, pieces_in, bias, cos, sin, aux_q, aux_k, chunk=512):
    depth, tokens = xt.shape
    count = len(pieces_in)
    rows = depth // count
    total_pairs = pieces_in[0].shape[1] // 384
    width = pairs * 128
    tspec = pl.BlockSpec((128, tokens), lambda i, me: (i, 0))
    tshape = jax.ShapeDtypeStruct((width, tokens), BF)
    piece_specs = [
        pl.BlockSpec((rows, 128), lambda i, me, col=col: (0, first + i + col * total_pairs))
        for col in range(3)
        for _ in range(count)
    ]
    wspec = pl.BlockSpec((depth, 128), lambda i, me: (0, i))
    return pl.pallas_call(
        functools.partial(attn_fwd_kernel, chunk, count),
        grid_spec=pltpu.PrefetchScalarGridSpec(
            num_scalar_prefetch=1,
            grid=(pairs,),
            in_specs=[const_spec(xt.shape)]
            + piece_specs
            + [pl.BlockSpec((128, 3), lambda i, me: (first + i, 0))]
            + [const_spec(z.shape) for z in (cos, sin, aux_q, aux_k)],
            out_specs=[tspec] * 4
            + [pl.BlockSpec((1, 2, tokens), lambda i, me: (i, 0, 0))]
            + [wspec] * 3,
            scratch_shapes=[
                pltpu.VMEM((HEAD_DIM + AUX, tokens), F32),
                pltpu.VMEM((1, tokens), F32),
            ],
        ),
        out_shape=[tshape] * 4
        + [jax.ShapeDtypeStruct((pairs, 2, tokens), F32)]
        + [jax.ShapeDtypeStruct((depth, width), BF)] * 3,
        compiler_params=params(),
        cost_estimate=lasts(7 * pairs),
        name="attn_fwd",
    )(me, xt, *(list(pieces_in) * 3), bias, cos, sin, aux_q, aux_k)


def norm_stats(r):
    center = r - jnp.mean(r, axis=-1, keepdims=True)
    rstd = lax.rsqrt(jnp.mean(center * center, axis=-1, keepdims=True) + 1e-5)
    return center * rstd, rstd


def norm_back(dyg, xhat, rstd):
    return rstd * (
        dyg
        - jnp.mean(dyg, axis=-1, keepdims=True)
        - xhat * jnp.mean(dyg * xhat, axis=-1, keepdims=True)
    )


def pl_reciprocal(d):
    return pltpu.reciprocal(d, approx=True)


def gelu_parts(u):
    e = jnp.exp2(u * u * (-0.5 * LOG2E))
    d = 1.0 + jnp.abs(u) * (ERFC_P * 0.7071067811865476)
    t = pl_reciprocal(d)
    t = t * (2.0 - d * t)
    poly = jnp.full_like(u, 0.5 * ERFC_C[-1])
    for coef in ERFC_C[-2::-1]:
        poly = poly * t + 0.5 * coef
    tail = poly * t * e
    phi_cum = jnp.where(u < 0, tail, 1.0 - tail)
    return u * phi_cum, phi_cum + u * (e * 0.3989422804014327)


def colsum(z):
    return jnp.sum(z, axis=0, keepdims=True)


def rows_kernel(count, me, x, ot, cot, vec, bu, *refs):
    pieces_in, refs = refs[: 4 * count], refs[4 * count :]
    y, gb_ref, dub_ref, h1b_ref, dfb_ref, dab_ref, dobt, small, dbu, wo, wu, wd, sems = refs

    wo, wu, wd = (w.reshape(w.shape[0] * 8, w.shape[2]) for w in (wo, wu, wd))
    half = wu.shape[1] // 2
    copies = []
    for col, w in enumerate((wo, wu, wu, wd)):
        for j in range(count):
            piece = pieces_in[col * count + j]
            rows = piece.shape[0]
            spot = pl.ds(pl.multiple_of((me[0] ^ j) * rows, rows), rows)
            if w is wu:
                at = pl.multiple_of((me[1] ^ (col - 1)) * half, half)
                place = w.at[spot, pl.ds(at, half)]
            else:
                place = w.at[spot, :]
            copies.append(pltpu.make_async_copy(piece, place, sems.at[col, j]))

    @pl.when(pl.program_id(0) == 0)
    def _():
        for copy in copies:
            copy.start()

    def arrived(first, last):
        @pl.when(pl.program_id(0) == 0)
        def _():
            for copy in copies[first * count : last * count]:
                copy.wait()

    arrived(0, 1)
    bo, bd = vec[0:1, :], vec[1:2, :]
    g1, c1, g2, c2 = vec[2:3, :], vec[3:4, :], vec[4:5, :], vec[5:6, :]
    a = dot(ot[...], wo[...], TN) + bo
    xhat1, rstd1 = norm_stats(x[...].astype(F32) + a)
    h1 = xhat1 * g1 + c1
    h1b = h1.astype(BF)
    h1b_ref[...] = h1b
    arrived(1, 3)
    u = dot(h1b, wu[...]) + bu[...]
    g, slope = gelu_parts(u)
    gb = g.astype(BF)
    gb_ref[...] = gb
    arrived(3, 4)
    f = dot(gb, wd[...]) + bd
    xhat2, rstd2 = norm_stats(h1 + f)
    y[...] = (xhat2 * g2 + c2).astype(BF)
    dy = cot[...].astype(F32)
    dr2 = norm_back(dy * g2, xhat2, rstd2)
    dfb = dr2.astype(BF)
    dfb_ref[...] = dfb
    dub = (dot(dfb, wd[...], NT) * slope).astype(BF)
    dub_ref[...] = dub
    dh1 = dr2 + dot(dub, wu[...], NT)
    dr1 = norm_back(dh1 * g1, xhat1, rstd1)
    dab = dr1.astype(BF)
    dab_ref[...] = dab
    dobt[...] = dot(wo[...], dab, NT).astype(BF)
    part = jnp.concatenate(
        [
            colsum(dab.astype(F32)),
            colsum(dfb.astype(F32)),
            colsum(dh1 * xhat1),
            colsum(dh1),
            colsum(dy * xhat2),
            colsum(dy),
            jnp.zeros((2, dy.shape[1]), F32),
        ],
        axis=0,
    )
    dbu_part = colsum(dub.astype(F32))

    @pl.when(pl.program_id(0) == 0)
    def _():
        small[...] = part
        dbu[...] = dbu_part

    @pl.when(pl.program_id(0) > 0)
    def _():
        small[...] += part
        dbu[...] += dbu_part


def rows_pass(me, x, ot, cot, wo, wu, wd, vec, bu, block=512):
    tokens, depth = x.shape
    wide = wu[0].shape[1] * 2
    count = len(wo)
    assert len(wu) == 2 * count
    row = pl.BlockSpec((block, depth), lambda i, me: (i, 0))
    row_wide = pl.BlockSpec((block, wide), lambda i, me: (i, 0))
    col = pl.BlockSpec((depth, block), lambda i, me: (0, i))
    narrow = jax.ShapeDtypeStruct((tokens, depth), BF)
    broad = jax.ShapeDtypeStruct((tokens, wide), BF)
    return pl.pallas_call(
        functools.partial(rows_kernel, count),
        grid_spec=pltpu.PrefetchScalarGridSpec(
            num_scalar_prefetch=1,
            grid=(tokens // block,),
            in_specs=[row, col, row]
            + [const_spec(z.shape) for z in (vec, bu)]
            + [pl.BlockSpec(memory_space=pl.ANY)] * (4 * count),
            out_specs=[row, row_wide, row_wide, row, row, row, col]
            + [const_spec((8, depth)), const_spec((1, wide))],
            scratch_shapes=[
                pltpu.VMEM((depth // 8, 8, depth), BF),
                pltpu.VMEM((depth // 8, 8, wide), BF),
                pltpu.VMEM((wide // 8, 8, depth), BF),
                pltpu.SemaphoreType.DMA((4, count)),
            ],
        ),
        out_shape=[
            narrow, broad, broad, narrow, narrow, narrow,
            jax.ShapeDtypeStruct((depth, tokens), BF),
            jax.ShapeDtypeStruct((8, depth), F32),
            jax.ShapeDtypeStruct((1, wide), F32),
        ],
        compiler_params=params(),
        cost_estimate=lasts(68),
        name="rows_pass",
    )(me, x, ot, cot, vec, bu, *wo, *wu, *wd)


def up_kernel(count, rows, me, h1b, dub, *refs):
    outs, result = refs[:count], refs[count]
    result[...] = dot(h1b[...], dub[...], TN)
    for j in range(count):
        spot = pl.ds(pl.multiple_of((me[0] ^ j) * rows, rows), rows)
        outs[j][...] = result[spot, :].astype(BF)


def up_grads(me, h1b, dub, count):
    tokens, depth = h1b.shape
    tiles = dub.shape[1] // depth
    rows = depth // count
    return pl.pallas_call(
        functools.partial(up_kernel, count, rows),
        grid_spec=pltpu.PrefetchScalarGridSpec(
            num_scalar_prefetch=1,
            grid=(tiles,),
            in_specs=[const_spec(h1b.shape), pl.BlockSpec((tokens, depth), lambda s, me: (0, s))],
            out_specs=[pl.BlockSpec((rows, depth), lambda s, me: (s, 0))] * count,
            scratch_shapes=[pltpu.VMEM((depth, depth), F32)],
        ),
        out_shape=[jax.ShapeDtypeStruct((tiles * rows, depth), BF)] * count,
        compiler_params=params(),
        cost_estimate=lasts(12),
        name="up_grads",
    )(me, h1b, dub)


def down_kernel(count, tiles, step_rows, me, gb, dfb, ot, dab, small, dbu, *refs):
    outs, result = refs[:count], refs[count]
    s = pl.program_id(0)
    height, depth = step_rows // count * tiles, dfb.shape[1]
    rows = depth // count

    @pl.when(s < tiles)
    def _():
        result[...] = dot(gb[...], dfb[...], TN)

    for t in range(tiles):
        per = step_rows // height if step_rows > height else 1

        @pl.when(s == t)
        def _():
            if per == 1:
                owner = t * step_rows // height
                at = t * step_rows % height
                for j in range(count):

                    @pl.when((me[0] ^ j) == owner)
                    def _():
                        outs[j][at : at + step_rows, :] = result[...].astype(BF)
            else:
                for i in range(per):
                    for j in range(count):

                        @pl.when((me[0] ^ j) == t * per + i)
                        def _():
                            part = result[i * height : (i + 1) * height, :]
                            outs[j][:height, :] = part.astype(BF)

    @pl.when(s == tiles)
    def _():
        result[...] = dot(ot[...], dab[...])
        wide = dbu.shape[1] // depth
        pad = jnp.zeros((16 - small.shape[0] - wide, depth), F32)
        lines = [small[...]] + [dbu[:, i * depth : (i + 1) * depth] for i in range(wide)] + [pad]
        lines = jnp.concatenate(lines, axis=0).astype(BF)
        for j in range(count):
            spot = pl.ds(pl.multiple_of((me[0] ^ j) * rows, rows), rows)
            outs[j][height : height + rows, :] = result[spot, :].astype(BF)
            outs[j][height + rows :, :] = lines


def down_out_grads(me, gb, dfb, ot, dab, small, dbu, count):
    tokens, wide = gb.shape
    depth = dfb.shape[1]
    tiles = wide // depth
    height = wide // count + depth // count + 16
    return pl.pallas_call(
        functools.partial(down_kernel, count, tiles, depth),
        grid_spec=pltpu.PrefetchScalarGridSpec(
            num_scalar_prefetch=1,
            grid=(tiles + 1,),
            in_specs=[pl.BlockSpec((tokens, depth), lambda s, me: (0, jnp.minimum(s, tiles - 1)))]
            + [const_spec(z.shape) for z in (dfb, ot, dab, small, dbu)],
            out_specs=[const_spec((height, depth))] * count,
            scratch_shapes=[pltpu.VMEM((depth, depth), F32)],
        ),
        out_shape=[jax.ShapeDtypeStruct((height, depth), BF)] * count,
        compiler_params=params(),
        cost_estimate=lasts(17),
        name="down_out_grads",
    )(me, gb, dfb, ot, dab, small, dbu)


def qkv_kernel(count, rows, spots, me, xt, *refs):
    ins, outs, result = refs[: 3 * len(spots)], refs[3 * len(spots) : -1], refs[-1]
    units = spots[-1][0] + 1
    unit = xt.shape[0] // 3
    for j in range(count):
        outs[j][units * rows :, :] = jnp.zeros_like(outs[j][units * rows :, :])
    ones = jnp.ones((16, xt.shape[1]), BF)
    line = lax.broadcasted_iota(jnp.int32, (16, 1), 0)
    for i, (u, at) in enumerate(spots):
        for t in range(3):
            d = ins[3 * i + t]
            columns = slice(t * unit + at, t * unit + at + d.shape[0])
            result[:, : d.shape[0]] = dot(xt[...], d[...], NT)
            bias = jnp.where(line == u, dot(ones, d[...], NT), 0.0).astype(BF)
            for j in range(count):
                spot = pl.ds(pl.multiple_of((me[0] ^ j) * rows, rows), rows)
                outs[j][u * rows : (u + 1) * rows, columns] = result[spot, : d.shape[0]].astype(BF)
                outs[j][units * rows :, columns] += bias


def qkv_grads(me, xt, triples, count):
    depth, tokens = xt.shape
    unit = depth // 3
    spots, at = [], 0
    for three in triples:
        spots.append((at // unit, at % unit))
        at += three[0].shape[0]
    flat = [z for three in triples for z in three]
    rows = depth // count
    shape = (at // unit * rows + 16, depth)
    return pl.pallas_call(
        functools.partial(qkv_kernel, count, rows, spots),
        grid_spec=pltpu.PrefetchScalarGridSpec(
            num_scalar_prefetch=1,
            grid=(1,),
            in_specs=[const_spec(z.shape) for z in [xt] + flat],
            out_specs=[const_spec(shape)] * count,
            scratch_shapes=[pltpu.VMEM((depth, unit), F32)],
        ),
        out_shape=[jax.ShapeDtypeStruct(shape, BF)] * count,
        compiler_params=params(),
        cost_estimate=lasts(4 * (at // unit) + 2),
        name="qkv_grads",
    )(me, xt, *flat)


def pieces(row):
    first = row.astype(BF)
    rest = row - first.astype(F32)
    second = rest.astype(BF)
    third = (rest - second.astype(F32)).astype(BF)
    return first.astype(F32), second.astype(F32), third.astype(F32)


def shift_rows(row, base):
    index = lax.broadcasted_iota(jnp.int32, (AUX, row.shape[1]), 0)
    out = base
    for i, piece in enumerate(pieces(row)):
        out = jnp.where(index == 3 + i, piece, out)
    return out.astype(BF)


def attn_bwd_kernel(chunk, qt, kt, vt, ot, dot_, lse, cos, sin, aux_q, aux_k, dqt, dkt, dvt, dq_acc):
    tokens = qt.shape[1]
    index = lax.broadcasted_iota(jnp.int32, (AUX, tokens), 0)
    aux_v = jnp.where((index >= 3) & (index < 6), 1.0, 0.0).astype(BF)
    for h in range(2):
        rows = slice(h * HEAD_DIM, (h + 1) * HEAD_DIM)
        q, k, v, do = qt[rows, :], kt[rows, :], vt[rows, :], dot_[rows, :]
        delta = jnp.sum(do.astype(F32) * ot[rows, :].astype(F32), axis=0, keepdims=True)
        qa = jnp.concatenate([q, shift_rows(-lse[0, h : h + 1, :], aux_q[...].astype(F32))], axis=0).T
        ka = jnp.concatenate([k, aux_k[...]], axis=0)
        da = jnp.concatenate([do, shift_rows(-delta, jnp.zeros((AUX, tokens), F32))], axis=0).T
        va = jnp.concatenate([v, aux_v], axis=0)
        dv = dk = None
        for c in range(tokens // chunk):
            sl = slice(c * chunk, (c + 1) * chunk)
            p = jnp.exp2(dot(qa[sl], ka))
            ds = (p * dot(da[sl], va)).astype(BF)
            dv_part = dot(do[:, sl], p.astype(BF))
            dk_part = dot(q[:, sl], ds)
            dv = dv_part if dv is None else dv + dv_part
            dk = dk_part if dk is None else dk + dk_part
            dq_acc[:, sl] = dot(k, ds, NT)
        dk = turn(dk * LN2, cos[...], -sin[...])
        dq = turn(dq_acc[...] * 0.125, cos[...], -sin[...])
        for out, value in ((dqt, dq), (dkt, dk), (dvt, dv)):
            out[rows, :] = value.astype(BF)


def attn_bwd(first, pairs, place, qt, kt, vt, ot, dobt, lse, cos, sin, aux_q, aux_k, chunk=256):
    tokens = qt.shape[1]
    ispec = pl.BlockSpec((128, tokens), lambda i: (i + first, 0))
    tspec = pl.BlockSpec((128, tokens), lambda i: (i, 0))
    tshape = jax.ShapeDtypeStruct((128 * pairs, tokens), BF)
    return pl.pallas_call(
        functools.partial(attn_bwd_kernel, chunk),
        grid=(pairs,),
        in_specs=[ispec] * 4
        + [pl.BlockSpec((128, tokens), lambda i: (i + place, 0))]
        + [pl.BlockSpec((1, 2, tokens), lambda i: (i + first, 0, 0))]
        + [const_spec(z.shape) for z in (cos, sin, aux_q, aux_k)],
        out_specs=[tspec] * 3,
        out_shape=[tshape] * 3,
        scratch_shapes=[pltpu.VMEM((HEAD_DIM, tokens), F32)],
        compiler_params=params(),
        cost_estimate=lasts(12 * pairs),
        name="attn_bwd",
    )(qt, kt, vt, ot, dobt, lse, cos, sin, aux_q, aux_k)


def token_kernel(units, dab, *refs):
    wq, wk, wv, out = refs[3 * units :]
    total = dab[...].astype(F32)
    at = 0
    for i in range(units):
        sl = slice(at, at + refs[3 * i].shape[0])
        at = sl.stop
        for d, w in zip(refs[3 * i : 3 * i + 3], (wq, wk, wv)):
            total = total + lax.dot_general(
                d[...], w[:, sl], (((0,), (1,)), ((), ())), preferred_element_type=F32
            )
    out[...] = total.astype(BF)


def token_grad_pass(dab, units, wq, wk, wv, block=512):
    tokens, depth = dab.shape
    row = pl.BlockSpec((block, depth), lambda i: (i, 0))
    flat = [z for unit in units for z in unit]
    return pl.pallas_call(
        functools.partial(token_kernel, len(units)),
        grid=(tokens // block,),
        in_specs=[row]
        + [pl.BlockSpec((z.shape[0], block), lambda i: (0, i)) for z in flat]
        + [const_spec(z.shape) for z in (wq, wk, wv)],
        out_specs=row,
        out_shape=jax.ShapeDtypeStruct((tokens, depth), BF),
        compiler_params=params(),
        cost_estimate=lasts(10),
        name="token_grad",
    )(dab, *flat, wq, wk, wv)


def join_halves(side, value, other, full):
    half = value.shape[1]
    full[:, pl.ds(pl.multiple_of(side * half, half), half)] = value[...].astype(F32)
    full[:, pl.ds(pl.multiple_of((1 - side) * half, half), half)] = other[...].astype(F32)


def finish_kernel(plan, count, side, *refs):
    ins, refs = refs[: 2 * count], refs[2 * count :]
    outs, full = refs[: len(plan)], refs[len(plan) :]
    for i in range(count):
        value, other = ins[2 * i], ins[2 * i + 1]
        if value.shape[1] < full[i].shape[1]:
            join_halves(side[0], value, other, full[i])
        else:
            full[i][...] = value[...].astype(F32) + other[...].astype(F32)
    for out, blocks in zip(outs, plan):
        for (i, row, column), (height, width), (to_row, to_column) in blocks:
            out[to_row : to_row + height, to_column : to_column + width] = full[i][
                row : row + height, column : column + width
            ]


def finish(side, pairs, depth, plan):
    sizes = []
    for blocks in plan:
        sizes.append(tuple(max(b[2][d] + b[1][d] for b in blocks) for d in range(2)))
    flat = [z for pair in pairs for z in pair]
    return pl.pallas_call(
        functools.partial(finish_kernel, plan, len(pairs)),
        grid_spec=pltpu.PrefetchScalarGridSpec(
            num_scalar_prefetch=1,
            grid=(1,),
            in_specs=[const_spec(z.shape) for z in flat],
            out_specs=[const_spec(z) for z in sizes],
            scratch_shapes=[pltpu.VMEM((pair[0].shape[0], depth), F32) for pair in pairs],
        ),
        out_shape=[jax.ShapeDtypeStruct(z, F32) for z in sizes],
        compiler_params=params(),
        cost_estimate=lasts(3),
        name="finish",
    )(side, *flat)


def swap(z, axis, bit):
    size = lax.axis_size(axis)
    return lax.ppermute(z, axis, [(i, i ^ bit) for i in range(size)])


def bits_of(size):
    return [1 << k for k in range(size.bit_length() - 1)]


def after(values, *deps):
    return lax.optimization_barrier((values, deps))[0]


def far_pieces(z):
    held = {0: z}
    for bit in reversed(bits_of(lax.axis_size("fsdp"))[1:]):
        held.update({j | bit: swap(piece, "fsdp", bit) for j, piece in list(held.items())})
    return held


def near_pieces(held):
    held = dict(held)
    held.update({j | 1: swap(piece, "fsdp", 1) for j, piece in list(held.items())})
    return [held[j] for j in range(len(held))]


def own_order(z, me):
    for bit in bits_of(z.shape[0]):
        flipped = z.reshape(-1, 2, bit, *z.shape[1:])[:, ::-1].reshape(z.shape)
        z = jnp.where((me & bit) == 0, z, flipped)
    return z


def total(terms):
    out = terms[0].astype(F32)
    for term in terms[1:]:
        out = out + term.astype(F32)
    return out


class Sums:
    def __init__(self):
        self.sent = []

    def swap(self, z, axis, bit):
        self.sent.append(z)
        return swap(z, axis, bit)

    def near(self, parts):
        terms = {j: [part] for j, part in enumerate(parts)}
        for j in [j for j in terms if j & 1]:
            terms[j ^ 1].append(self.swap(terms.pop(j)[0], "fsdp", 1))
        return terms

    def far(self, terms):
        terms = dict(terms)
        for bit in bits_of(lax.axis_size("fsdp"))[1:]:
            for j in [j for j in terms if j & bit]:
                value = total(terms.pop(j)).astype(BF)
                terms[j ^ bit] = terms[j ^ bit] + [self.swap(value, "fsdp", bit)]
        return terms[0]

    def halves(self, terms):
        half = terms[0].shape[1] // 2
        side = lax.axis_index("dp") % 2
        away = [lax.dynamic_slice_in_dim(t, (1 - side) * half, half, 1) for t in terms]
        here = [lax.dynamic_slice_in_dim(t, side * half, half, 1) for t in terms]
        return here + [self.swap(total(away).astype(BF), "dp", 1)]

    def pair_up(self, terms, bit):
        value = total(terms).astype(BF)
        return [value, self.swap(value, "dp", bit)]


def shards(
    tokens, cotangent, bucket, key_lengths,
    query_weight, key_weight, value_weight, output_weight, up_weight, down_weight,
    query_bias, key_bias, value_bias, output_bias, up_bias, down_bias,
    first_gain, first_shift, second_gain, second_shift,
):
    count = lax.axis_size("fsdp")
    me_scalar = lax.axis_index("fsdp").astype(jnp.int32)
    me = me_scalar[None]
    row_count, depth = tokens.shape
    rows = depth // count
    wide_rows = up_bias.shape[0]

    dp_size = lax.axis_size("dp")
    side = (lax.axis_index("dp") % 2).astype(jnp.int32)[None]
    pairs = depth // 128
    cut = pairs // 3
    qkv1, qkv2 = pack(query_weight, key_weight, value_weight, cut * 128)
    names = (
        query_bias, key_bias, value_bias, output_bias, down_bias,
        first_gain, first_shift, second_gain, second_shift, up_bias,
    )
    names = after(names, qkv1)
    narrow = jnp.stack([jnp.pad(z, (0, wide_rows - rows)) for z in names[:9]] + [names[9]])
    narrow = jnp.pad(narrow, ((0, 6), (0, 0)))
    qkv1 = far_pieces(qkv1)
    qkv2 = far_pieces(qkv2)
    thin = near_pieces(far_pieces(narrow))
    up_here, up_away = split(side, after(up_weight, narrow))
    aux_q, aux_k, cos, sin = layout_tables(after(bucket, up_here)[0], key_lengths[0], row_count)
    xt = after(tokens, up_here).T
    qkv1 = near_pieces(after(qkv1, xt, aux_q, aux_k, cos, sin))
    up_here = after(up_here, list(qkv1))
    wu_here = far_pieces(up_here)

    thin = own_order(jnp.stack(thin), me_scalar).astype(F32)
    vectors = thin[:, :9, :rows].transpose(1, 0, 2).reshape(9, depth)
    bu = thin[:, 9].reshape(1, -1)
    bias3 = vectors[:3].T
    vec = jnp.pad(vectors[3:], ((0, 2), (0, 0)))

    tables = (cos, sin, aux_q, aux_k)
    bias2 = bias3[cut * 128 :]
    fwd = [attn_fwd(me, 0, cut, xt, qkv1, bias3[: cut * 128], *tables)]
    qkv2 = near_pieces(after(qkv2, fwd[0][0]))
    out_w, down_w = after((output_weight, down_weight), list(qkv2))
    wo = far_pieces(out_w)
    wd = far_pieces(down_w)
    fwd.append(attn_fwd(me, 0, cut, after(xt, out_w, down_w), qkv2, bias2, *tables))
    wu_here = after(wu_here, fwd[1][0])
    wu_away = {0: up_away}
    wu_away.update({j: swap(z, "dp", 1) for j, z in wu_here.items() if j})
    fwd.append(
        attn_fwd(me, cut, cut, after(xt, list(wu_here.values())), qkv2, bias2, *tables)
    )
    wo, wd, wu_away = after((wo, wd, wu_away), fwd[2][0])
    wu_here, wo, wd, wu_away = (near_pieces(z) for z in (wu_here, wo, wd, wu_away))
    ot = jnp.concatenate([z[3] for z in fwd], axis=0)
    wq, wk, wv = (jnp.concatenate([z[i] for z in fwd], axis=1) for i in (5, 6, 7))
    who = jnp.concatenate([me, side])
    y, gb, dub, h1b, dfb, dab, dobt, small, dbu = rows_pass(
        who, tokens, ot, cotangent, wo, wu_here + wu_away, wd, vec, bu
    )

    sums = Sums()
    done = []

    def then(terms):
        return after(terms, done)

    u_parts = up_grads(me, h1b, dub, count)
    u_terms = sums.near(u_parts)
    d_parts = down_out_grads(me, after(gb, u_parts), dfb, ot, dab, small, dbu, count)
    done[:] = [d_parts[0]]
    u_terms = sums.far(then(u_terms))
    d_terms = sums.near(d_parts)

    rest = bits_of(dp_size)[1:]
    lines = [list(range(i, dp_size, 2)) for i in range(2)]

    def backward(i, many):
        part = fwd[i // cut]
        args = after((*part[:4], dobt), sums.sent, done)
        out = attn_bwd(i % cut, many, i, *args, part[4], cos, sin, aux_q, aux_k)
        done[:] = [out[0]]
        return out

    def units(outs):
        args = after(outs, sums.sent)
        parts = qkv_grads(me, xt, args, count)
        done[:] = [parts[0]]
        return parts

    def line_gather(terms):
        return lax.all_gather(total(terms).astype(BF), "dp", axis_index_groups=lines)

    def line_sum(stack):
        return jnp.sum(stack.astype(F32), axis=0).astype(BF)

    def other_half(value):
        return (value, sums.swap(value, "dp", 1))

    back = [backward(0, 2)]
    u_terms = sums.halves(then(u_terms))
    d_terms = sums.far(then(d_terms))
    back.append(backward(2, 1))
    u_value = line_gather(then(u_terms))
    back.append(backward(3, 1))
    d_terms = sums.halves(then(d_terms))
    a_terms = sums.near(units(back))
    back.append(backward(4, 1))
    a_terms = sums.far(then(a_terms))
    d_value = line_gather(after(d_terms, done, u_value))
    back.append(backward(5, 1))
    a_terms = sums.halves(then(a_terms))
    u_pair = other_half(line_sum(then(u_value)))
    c_terms = sums.near(units(back[3:]))
    a_terms = sums.pair_up(then(a_terms), rest[0])
    c_terms = sums.far(then(c_terms))
    dab = after(dab, sums.sent, done)
    token_grad = token_grad_pass(dab, back, wq, wk, wv)
    done[:] = [token_grad]
    c_terms = sums.pair_up(then(c_terms), 1)
    for bit in rest[1:]:
        a_terms = sums.pair_up(then(a_terms), bit)
    d_pair = other_half(line_sum(then(d_value)))
    for bit in rest:
        c_terms = sums.pair_up(c_terms, bit)
    a_pair = other_half(total(a_terms).astype(BF))

    tiles = up_weight.shape[1] // depth
    height = down_weight.shape[0]
    unit = depth // 3
    place = [(0, 0), (0, rows), (1, 0)]
    (d_up,) = finish(
        side, [u_pair], depth,
        [[((0, t * rows, 0), (rows, depth), (0, t * depth)) for t in range(tiles)]],
    )
    d_down, d_out, thin = finish(
        side, [d_pair], depth,
        [
            [((0, 0, 0), (height, depth), (0, 0))],
            [((0, height, 0), (rows, depth), (0, 0))],
            [((0, height + rows, 0), (16, depth), (0, 0))],
        ],
    )
    d_q, d_k, d_v, bias = finish(
        side, [a_pair, c_terms], depth,
        [
            [((i, row, t * unit), (rows, unit), (0, u * unit)) for u, (i, row) in enumerate(place)]
            for t in range(3)
        ]
        + [[((0, 2 * rows, 0), (16, depth), (0, 0)), ((1, rows, 0), (16, depth), (16, 0))]],
    )

    def own(z):
        return lax.dynamic_slice_in_dim(z, me_scalar * rows, rows, z.ndim - 1)

    b_o, b_d, gain1, shift1, gain2, shift2 = own(thin[:6])
    b_up = lax.dynamic_slice_in_dim(thin[8 : 8 + tiles].reshape(-1), me_scalar * wide_rows, wide_rows, 0)
    bias = jnp.stack([bias[0], bias[1], bias[16]]).reshape(3, 3, unit).transpose(1, 0, 2)
    b_q, b_k, b_v = own(bias.reshape(3, depth))
    return (
        y, token_grad, d_q, d_k, d_v, d_out, d_up, d_down,
        b_q, b_k, b_v, b_o, b_up, b_d, gain1, shift1, gain2, shift2,
    )


def solution(mesh):
    rows = P(("dp", "fsdp"), None)
    mat = P("fsdp", None)
    vector = P("fsdp")
    in_specs = (rows, rows, P(("dp", "fsdp")), rows) + (mat,) * 6 + (vector,) * 10
    out_specs = (rows, rows) + (mat,) * 6 + (vector,) * 10
    return jax.shard_map(shards, mesh=mesh, in_specs=in_specs, out_specs=out_specs, check_vma=False)
```

```python
import functools

import jax
import jax.numpy as jnp
from jax import lax
from jax.experimental import pallas as pl
from jax.experimental.pallas import tpu as pltpu
from jax.sharding import PartitionSpec as P

HEAD_DIM = 64
HALF = 32
SLOT = 512
AUX = 16
NEG = -1e30
LOG2E = 1.4426950408889634
LN2 = 0.6931471805599453
QSCALE = 0.125 * LOG2E
BF = jnp.bfloat16
F32 = jnp.float32
NN = ((1,), (0,))
NT = ((1,), (1,))
TN = ((0,), (0,))
ERFC_P = 0.37
ERFC_C = (
    0.20835304049472436,
    0.2152118908535975,
    0.15105251587527643,
    0.3213824037594925,
    -0.19174412290346565,
    0.4392956874015427,
    -0.14355086909593573,
)
VMEM_LIMIT = 60 << 20


def lasts(us):
    return pl.CostEstimate(flops=us * 1000000000, bytes_accessed=us * 3000000, transcendentals=0)


def dot(a, b, dims=NN):
    return lax.dot_general(a, b, (dims, ((), ())), preferred_element_type=F32)


def params(**kw):
    return pltpu.CompilerParams(vmem_limit_bytes=VMEM_LIMIT, **kw)


def const_spec(shape):
    return pl.BlockSpec(shape, lambda *_: (0,) * len(shape), pipeline_mode=pl.Buffered(1))


def layout_tables(bucket_value, lengths_row, row_count):
    places = jnp.arange(row_count, dtype=jnp.int32)
    slot_index = places // SLOT
    sequence = jnp.where(
        bucket_value == 0, slot_index, jnp.where(bucket_value == 1, slot_index // 2, 0)
    )
    starts = jnp.where(
        bucket_value == 0,
        slot_index * SLOT,
        jnp.where(bucket_value == 1, slot_index // 2 * 2 * SLOT, 0),
    )
    offsets = places - starts
    limits = jnp.zeros_like(places)
    for member in range(3):
        limits = limits + jnp.where(sequence == member, lengths_row[member], 0)
    valid = offsets < limits
    rows = jnp.arange(AUX, dtype=jnp.int32)[:, None]
    same = (rows == sequence[None, :]) & (rows < 3)
    aux_q = jnp.where(same, 1.0, 0.0).astype(BF)
    aux_k = jnp.where(
        rows < 3,
        jnp.where(same & valid[None, :], 0.0, NEG),
        jnp.where(rows < 6, 1.0, 0.0),
    ).astype(BF)
    exponents = jnp.arange(HALF, dtype=F32) * (-2.0 / HEAD_DIM)
    inverse = jnp.power(jnp.float32(10000.0), exponents)
    angles = inverse[:, None] * offsets.astype(F32)[None, :]
    return aux_q, aux_k, jnp.cos(angles), jnp.sin(angles)


def turn(z, cos, sin):
    a, b = z[:HALF], z[HALF:]
    return jnp.concatenate([a * cos - b * sin, b * cos + a * sin], axis=0)


def pack_kernel(cut, wq, wk, wv, one, two):
    depth = wq.shape[1]
    for t, w in enumerate((wq, wk, wv)):
        one[:, t * cut : (t + 1) * cut] = w[:, :cut]
        two[:, t * (depth - cut) : (t + 1) * (depth - cut)] = w[:, cut:]


def pack(wq, wk, wv, cut):
    rows, depth = wq.shape
    sizes = [(rows, 3 * cut), (rows, 3 * (depth - cut))]
    return pl.pallas_call(
        functools.partial(pack_kernel, cut),
        grid=(1,),
        in_specs=[const_spec(wq.shape)] * 3,
        out_specs=[const_spec(z) for z in sizes],
        out_shape=[jax.ShapeDtypeStruct(z, BF) for z in sizes],
        compiler_params=params(),
        cost_estimate=lasts(2),
        name="pack",
    )(wq, wk, wv)


def split_kernel(side, w, here, away):
    half = here.shape[1]
    here[...] = w[:, pl.ds(pl.multiple_of(side[0] * half, half), half)]
    away[...] = w[:, pl.ds(pl.multiple_of((1 - side[0]) * half, half), half)]


def split(side, w):
    rows, wide = w.shape
    size = (rows, wide // 2)
    return pl.pallas_call(
        split_kernel,
        grid_spec=pltpu.PrefetchScalarGridSpec(
            num_scalar_prefetch=1,
            grid=(1,),
            in_specs=[const_spec(w.shape)],
            out_specs=[const_spec(size)] * 2,
        ),
        out_shape=[jax.ShapeDtypeStruct(size, BF)] * 2,
        compiler_params=params(),
        cost_estimate=lasts(2),
        name="split",
    )(side, w)


def attn_fwd_kernel(chunk, count, me, xt, *refs):
    pieces_in, refs = refs[: 3 * count], refs[3 * count :]
    bias, cos, sin, aux_q, aux_k, qt, kt, vt, ot, lse, wq, wk, wv, acc, top = refs
    tokens = xt.shape[1]
    x = xt[...]
    for col, (w, out) in enumerate(((wq, qt), (wk, kt), (wv, vt))):
        for j in range(count):
            piece = pieces_in[col * count + j]
            rows = piece.shape[0]
            w[pl.ds(pl.multiple_of((me[0] ^ j) * rows, rows), rows), :] = piece[...]
        z = dot(w[...], x, TN) + bias[:, col : col + 1]
        if col == 2:
            out[...] = z.astype(BF)
            continue
        for h in range(2):
            r = turn(z[h * HEAD_DIM : (h + 1) * HEAD_DIM], cos[...], sin[...])
            if col == 0:
                r = r * QSCALE
            out[h * HEAD_DIM : (h + 1) * HEAD_DIM, :] = r.astype(BF)
    ones = jnp.ones((AUX, tokens), BF)
    for h in range(2):
        rows = slice(h * HEAD_DIM, (h + 1) * HEAD_DIM)
        q32 = qt[rows, :].astype(F32)
        k32 = kt[rows, :].astype(F32)
        bound = jnp.max(jnp.sum(q32 * q32, axis=0)) * jnp.max(jnp.sum(k32 * k32, axis=0))
        qa = jnp.concatenate([qt[rows, :], aux_q[...]], axis=0)
        ka = jnp.concatenate([kt[rows, :], aux_k[...]], axis=0).T
        va = jnp.concatenate([vt[rows, :], ones], axis=0)
        small = bound < 8100.0

        @pl.when(small)
        def _():
            total = None
            for c in range(tokens // chunk):
                sl = slice(c * chunk, (c + 1) * chunk)
                p = jnp.exp2(dot(ka[sl], qa)).astype(BF)
                part = dot(va[:, sl], p)
                total = part if total is None else total + part
            acc[...] = total
            top[...] = jnp.zeros_like(top)

        @pl.when(jnp.logical_not(small))
        def _():
            total = None
            for c in range(tokens // chunk):
                sl = slice(c * chunk, (c + 1) * chunk)
                s = dot(ka[sl], qa)
                here = jnp.max(s, axis=0, keepdims=True)
                if c == 0:
                    best = here
                    total = dot(va[:, sl], jnp.exp2(s - best).astype(BF))
                else:
                    later = jnp.maximum(best, here)
                    part = dot(va[:, sl], jnp.exp2(s - later).astype(BF))
                    total = total * jnp.exp2(best - later) + part
                    best = later
            acc[...] = total
            top[...] = best

        row_total = acc[HEAD_DIM : HEAD_DIM + 1, :]
        ot[rows, :] = (acc[:HEAD_DIM, :] / row_total).astype(BF)
        lse[0, h : h + 1, :] = top[...] + jnp.log2(row_total)


def attn_fwd(me, first, pairs, xt, pieces_in, bias, cos, sin, aux_q, aux_k, chunk=512):
    depth, tokens = xt.shape
    count = len(pieces_in)
    rows = depth // count
    total_pairs = pieces_in[0].shape[1] // 384
    width = pairs * 128
    tspec = pl.BlockSpec((128, tokens), lambda i, me: (i, 0))
    tshape = jax.ShapeDtypeStruct((width, tokens), BF)
    piece_specs = [
        pl.BlockSpec((rows, 128), lambda i, me, col=col: (0, first + i + col * total_pairs))
        for col in range(3)
        for _ in range(count)
    ]
    wspec = pl.BlockSpec((depth, 128), lambda i, me: (0, i))
    return pl.pallas_call(
        functools.partial(attn_fwd_kernel, chunk, count),
        grid_spec=pltpu.PrefetchScalarGridSpec(
            num_scalar_prefetch=1,
            grid=(pairs,),
            in_specs=[const_spec(xt.shape)]
            + piece_specs
            + [pl.BlockSpec((128, 3), lambda i, me: (first + i, 0))]
            + [const_spec(z.shape) for z in (cos, sin, aux_q, aux_k)],
            out_specs=[tspec] * 4
            + [pl.BlockSpec((1, 2, tokens), lambda i, me: (i, 0, 0))]
            + [wspec] * 3,
            scratch_shapes=[
                pltpu.VMEM((HEAD_DIM + AUX, tokens), F32),
                pltpu.VMEM((1, tokens), F32),
            ],
        ),
        out_shape=[tshape] * 4
        + [jax.ShapeDtypeStruct((pairs, 2, tokens), F32)]
        + [jax.ShapeDtypeStruct((depth, width), BF)] * 3,
        compiler_params=params(),
        cost_estimate=lasts(7 * pairs),
        name="attn_fwd",
    )(me, xt, *(list(pieces_in) * 3), bias, cos, sin, aux_q, aux_k)


def norm_stats(r):
    center = r - jnp.mean(r, axis=-1, keepdims=True)
    rstd = lax.rsqrt(jnp.mean(center * center, axis=-1, keepdims=True) + 1e-5)
    return center * rstd, rstd


def norm_back(dyg, xhat, rstd):
    return rstd * (
        dyg
        - jnp.mean(dyg, axis=-1, keepdims=True)
        - xhat * jnp.mean(dyg * xhat, axis=-1, keepdims=True)
    )


def pl_reciprocal(d):
    return pltpu.reciprocal(d, approx=True)


def gelu_parts(u):
    e = jnp.exp2(u * u * (-0.5 * LOG2E))
    d = 1.0 + jnp.abs(u) * (ERFC_P * 0.7071067811865476)
    t = pl_reciprocal(d)
    t = t * (2.0 - d * t)
    poly = jnp.full_like(u, 0.5 * ERFC_C[-1])
    for coef in ERFC_C[-2::-1]:
        poly = poly * t + 0.5 * coef
    tail = poly * t * e
    phi_cum = jnp.where(u < 0, tail, 1.0 - tail)
    return u * phi_cum, phi_cum + u * (e * 0.3989422804014327)


def colsum(z):
    return jnp.sum(z, axis=0, keepdims=True)


def rows_kernel(count, me, x, ot, cot, vec, bu, *refs):
    pieces_in, refs = refs[: 4 * count], refs[4 * count :]
    y, gb_ref, dub_ref, h1b_ref, dfb_ref, dab_ref, dobt, small, dbu, wo, wu, wd, sems = refs

    wo, wu, wd = (w.reshape(w.shape[0] * 8, w.shape[2]) for w in (wo, wu, wd))
    half = wu.shape[1] // 2
    copies = []
    for col, w in enumerate((wo, wu, wu, wd)):
        for j in range(count):
            piece = pieces_in[col * count + j]
            rows = piece.shape[0]
            spot = pl.ds(pl.multiple_of((me[0] ^ j) * rows, rows), rows)
            if w is wu:
                at = pl.multiple_of((me[1] ^ (col - 1)) * half, half)
                place = w.at[spot, pl.ds(at, half)]
            else:
                place = w.at[spot, :]
            copies.append(pltpu.make_async_copy(piece, place, sems.at[col, j]))

    @pl.when(pl.program_id(0) == 0)
    def _():
        for copy in copies:
            copy.start()

    def arrived(first, last):
        @pl.when(pl.program_id(0) == 0)
        def _():
            for copy in copies[first * count : last * count]:
                copy.wait()

    arrived(0, 1)
    bo, bd = vec[0:1, :], vec[1:2, :]
    g1, c1, g2, c2 = vec[2:3, :], vec[3:4, :], vec[4:5, :], vec[5:6, :]
    a = dot(ot[...], wo[...], TN) + bo
    xhat1, rstd1 = norm_stats(x[...].astype(F32) + a)
    h1 = xhat1 * g1 + c1
    h1b = h1.astype(BF)
    h1b_ref[...] = h1b
    arrived(1, 3)
    u = dot(h1b, wu[...]) + bu[...]
    g, slope = gelu_parts(u)
    gb = g.astype(BF)
    gb_ref[...] = gb
    arrived(3, 4)
    f = dot(gb, wd[...]) + bd
    xhat2, rstd2 = norm_stats(h1 + f)
    y[...] = (xhat2 * g2 + c2).astype(BF)
    dy = cot[...].astype(F32)
    dr2 = norm_back(dy * g2, xhat2, rstd2)
    dfb = dr2.astype(BF)
    dfb_ref[...] = dfb
    dub = (dot(dfb, wd[...], NT) * slope).astype(BF)
    dub_ref[...] = dub
    dh1 = dr2 + dot(dub, wu[...], NT)
    dr1 = norm_back(dh1 * g1, xhat1, rstd1)
    dab = dr1.astype(BF)
    dab_ref[...] = dab
    dobt[...] = dot(wo[...], dab, NT).astype(BF)
    part = jnp.concatenate(
        [
            colsum(dab.astype(F32)),
            colsum(dfb.astype(F32)),
            colsum(dh1 * xhat1),
            colsum(dh1),
            colsum(dy * xhat2),
            colsum(dy),
            jnp.zeros((2, dy.shape[1]), F32),
        ],
        axis=0,
    )
    dbu_part = colsum(dub.astype(F32))

    @pl.when(pl.program_id(0) == 0)
    def _():
        small[...] = part
        dbu[...] = dbu_part

    @pl.when(pl.program_id(0) > 0)
    def _():
        small[...] += part
        dbu[...] += dbu_part


def rows_pass(me, x, ot, cot, wo, wu, wd, vec, bu, block=512):
    tokens, depth = x.shape
    wide = wu[0].shape[1] * 2
    count = len(wo)
    assert len(wu) == 2 * count
    row = pl.BlockSpec((block, depth), lambda i, me: (i, 0))
    row_wide = pl.BlockSpec((block, wide), lambda i, me: (i, 0))
    col = pl.BlockSpec((depth, block), lambda i, me: (0, i))
    narrow = jax.ShapeDtypeStruct((tokens, depth), BF)
    broad = jax.ShapeDtypeStruct((tokens, wide), BF)
    return pl.pallas_call(
        functools.partial(rows_kernel, count),
        grid_spec=pltpu.PrefetchScalarGridSpec(
            num_scalar_prefetch=1,
            grid=(tokens // block,),
            in_specs=[row, col, row]
            + [const_spec(z.shape) for z in (vec, bu)]
            + [pl.BlockSpec(memory_space=pl.ANY)] * (4 * count),
            out_specs=[row, row_wide, row_wide, row, row, row, col]
            + [const_spec((8, depth)), const_spec((1, wide))],
            scratch_shapes=[
                pltpu.VMEM((depth // 8, 8, depth), BF),
                pltpu.VMEM((depth // 8, 8, wide), BF),
                pltpu.VMEM((wide // 8, 8, depth), BF),
                pltpu.SemaphoreType.DMA((4, count)),
            ],
        ),
        out_shape=[
            narrow, broad, broad, narrow, narrow, narrow,
            jax.ShapeDtypeStruct((depth, tokens), BF),
            jax.ShapeDtypeStruct((8, depth), F32),
            jax.ShapeDtypeStruct((1, wide), F32),
        ],
        compiler_params=params(),
        cost_estimate=lasts(68),
        name="rows_pass",
    )(me, x, ot, cot, vec, bu, *wo, *wu, *wd)


def up_kernel(count, rows, me, h1b, dub, *refs):
    outs, result = refs[:count], refs[count]
    result[...] = dot(h1b[...], dub[...], TN)
    for j in range(count):
        spot = pl.ds(pl.multiple_of((me[0] ^ j) * rows, rows), rows)
        outs[j][...] = result[spot, :].astype(BF)


def up_grads(me, h1b, dub, count):
    tokens, depth = h1b.shape
    tiles = dub.shape[1] // depth
    rows = depth // count
    return pl.pallas_call(
        functools.partial(up_kernel, count, rows),
        grid_spec=pltpu.PrefetchScalarGridSpec(
            num_scalar_prefetch=1,
            grid=(tiles,),
            in_specs=[const_spec(h1b.shape), pl.BlockSpec((tokens, depth), lambda s, me: (0, s))],
            out_specs=[pl.BlockSpec((rows, depth), lambda s, me: (s, 0))] * count,
            scratch_shapes=[pltpu.VMEM((depth, depth), F32)],
        ),
        out_shape=[jax.ShapeDtypeStruct((tiles * rows, depth), BF)] * count,
        compiler_params=params(),
        cost_estimate=lasts(12),
        name="up_grads",
    )(me, h1b, dub)


def down_kernel(count, tiles, step_rows, me, gb, dfb, ot, dab, small, dbu, *refs):
    outs, result = refs[:count], refs[count]
    s = pl.program_id(0)
    height, depth = step_rows // count * tiles, dfb.shape[1]
    rows = depth // count

    @pl.when(s < tiles)
    def _():
        result[...] = dot(gb[...], dfb[...], TN)

    for t in range(tiles):
        per = step_rows // height if step_rows > height else 1

        @pl.when(s == t)
        def _():
            if per == 1:
                owner = t * step_rows // height
                at = t * step_rows % height
                for j in range(count):

                    @pl.when((me[0] ^ j) == owner)
                    def _():
                        outs[j][at : at + step_rows, :] = result[...].astype(BF)
            else:
                for i in range(per):
                    for j in range(count):

                        @pl.when((me[0] ^ j) == t * per + i)
                        def _():
                            part = result[i * height : (i + 1) * height, :]
                            outs[j][:height, :] = part.astype(BF)

    @pl.when(s == tiles)
    def _():
        result[...] = dot(ot[...], dab[...])
        wide = dbu.shape[1] // depth
        pad = jnp.zeros((16 - small.shape[0] - wide, depth), F32)
        lines = [small[...]] + [dbu[:, i * depth : (i + 1) * depth] for i in range(wide)] + [pad]
        lines = jnp.concatenate(lines, axis=0).astype(BF)
        for j in range(count):
            spot = pl.ds(pl.multiple_of((me[0] ^ j) * rows, rows), rows)
            outs[j][height : height + rows, :] = result[spot, :].astype(BF)
            outs[j][height + rows :, :] = lines


def down_out_grads(me, gb, dfb, ot, dab, small, dbu, count):
    tokens, wide = gb.shape
    depth = dfb.shape[1]
    tiles = wide // depth
    height = wide // count + depth // count + 16
    return pl.pallas_call(
        functools.partial(down_kernel, count, tiles, depth),
        grid_spec=pltpu.PrefetchScalarGridSpec(
            num_scalar_prefetch=1,
            grid=(tiles + 1,),
            in_specs=[pl.BlockSpec((tokens, depth), lambda s, me: (0, jnp.minimum(s, tiles - 1)))]
            + [const_spec(z.shape) for z in (dfb, ot, dab, small, dbu)],
            out_specs=[const_spec((height, depth))] * count,
            scratch_shapes=[pltpu.VMEM((depth, depth), F32)],
        ),
        out_shape=[jax.ShapeDtypeStruct((height, depth), BF)] * count,
        compiler_params=params(),
        cost_estimate=lasts(17),
        name="down_out_grads",
    )(me, gb, dfb, ot, dab, small, dbu)


def joined(refs, sizes):
    units, at = [], 0
    for size in sizes:
        threes = [refs[3 * (at + i) : 3 * (at + i) + 3] for i in range(size)]
        units.append([jnp.concatenate([z[t][...] for z in threes], axis=0) for t in range(3)])
        at += size
    return units


def unit_sizes(triples, unit):
    sizes, width = [], unit
    for three in triples:
        if width == unit:
            sizes.append(0)
            width = 0
        sizes[-1] += 1
        width += three[0].shape[0]
    return tuple(sizes)


def qkv_kernel(count, rows, sizes, me, xt, *refs):
    ins, outs, result = refs[: 3 * sum(sizes)], refs[3 * sum(sizes) : -1], refs[-1]
    units = len(sizes)
    unit = xt.shape[0] // 3
    ones = jnp.ones((16, xt.shape[1]), BF)
    line = lax.broadcasted_iota(jnp.int32, (16, 1), 0)
    arrays = joined(ins, sizes)
    for t in range(3):
        columns = slice(t * unit, (t + 1) * unit)
        bias = jnp.zeros((16, unit), F32)
        for u in range(units):
            d = arrays[u][t]
            result[...] = dot(xt[...], d, NT)
            bias = bias + jnp.where(line == u, dot(ones, d, NT), 0.0)
            for j in range(count):
                spot = pl.ds(pl.multiple_of((me[0] ^ j) * rows, rows), rows)
                outs[j][u * rows : (u + 1) * rows, columns] = result[spot, :].astype(BF)
        for j in range(count):
            outs[j][units * rows :, columns] = bias.astype(BF)


def qkv_grads(me, xt, triples, count):
    depth, tokens = xt.shape
    unit = depth // 3
    sizes = unit_sizes(triples, unit)
    units = len(sizes)
    flat = [z for three in triples for z in three]
    rows = depth // count
    shape = (units * rows + 16, depth)
    return pl.pallas_call(
        functools.partial(qkv_kernel, count, rows, sizes),
        grid_spec=pltpu.PrefetchScalarGridSpec(
            num_scalar_prefetch=1,
            grid=(1,),
            in_specs=[const_spec(z.shape) for z in [xt] + flat],
            out_specs=[const_spec(shape)] * count,
            scratch_shapes=[pltpu.VMEM((depth, unit), F32)],
        ),
        out_shape=[jax.ShapeDtypeStruct(shape, BF)] * count,
        compiler_params=params(),
        cost_estimate=lasts(4 * units + 2),
        name="qkv_grads",
    )(me, xt, *flat)


def pieces(row):
    first = row.astype(BF)
    rest = row - first.astype(F32)
    second = rest.astype(BF)
    third = (rest - second.astype(F32)).astype(BF)
    return first.astype(F32), second.astype(F32), third.astype(F32)


def shift_rows(row, base):
    index = lax.broadcasted_iota(jnp.int32, (AUX, row.shape[1]), 0)
    out = base
    for i, piece in enumerate(pieces(row)):
        out = jnp.where(index == 3 + i, piece, out)
    return out.astype(BF)


def attn_bwd_kernel(chunk, qt, kt, vt, ot, dot_, lse, cos, sin, aux_q, aux_k, dqt, dkt, dvt, dq_acc):
    tokens = qt.shape[1]
    index = lax.broadcasted_iota(jnp.int32, (AUX, tokens), 0)
    aux_v = jnp.where((index >= 3) & (index < 6), 1.0, 0.0).astype(BF)
    for h in range(2):
        rows = slice(h * HEAD_DIM, (h + 1) * HEAD_DIM)
        q, k, v, do = qt[rows, :], kt[rows, :], vt[rows, :], dot_[rows, :]
        delta = jnp.sum(do.astype(F32) * ot[rows, :].astype(F32), axis=0, keepdims=True)
        qa = jnp.concatenate([q, shift_rows(-lse[0, h : h + 1, :], aux_q[...].astype(F32))], axis=0).T
        ka = jnp.concatenate([k, aux_k[...]], axis=0)
        da = jnp.concatenate([do, shift_rows(-delta, jnp.zeros((AUX, tokens), F32))], axis=0).T
        va = jnp.concatenate([v, aux_v], axis=0)
        dv = dk = None
        for c in range(tokens // chunk):
            sl = slice(c * chunk, (c + 1) * chunk)
            p = jnp.exp2(dot(qa[sl], ka))
            ds = (p * dot(da[sl], va)).astype(BF)
            dv_part = dot(do[:, sl], p.astype(BF))
            dk_part = dot(q[:, sl], ds)
            dv = dv_part if dv is None else dv + dv_part
            dk = dk_part if dk is None else dk + dk_part
            dq_acc[:, sl] = dot(k, ds, NT)
        dk = turn(dk * LN2, cos[...], -sin[...])
        dq = turn(dq_acc[...] * 0.125, cos[...], -sin[...])
        for out, value in ((dqt, dq), (dkt, dk), (dvt, dv)):
            out[rows, :] = value.astype(BF)


def attn_bwd(first, pairs, place, qt, kt, vt, ot, dobt, lse, cos, sin, aux_q, aux_k, chunk=256):
    tokens = qt.shape[1]
    ispec = pl.BlockSpec((128, tokens), lambda i: (i + first, 0))
    tspec = pl.BlockSpec((128, tokens), lambda i: (i, 0))
    tshape = jax.ShapeDtypeStruct((128 * pairs, tokens), BF)
    return pl.pallas_call(
        functools.partial(attn_bwd_kernel, chunk),
        grid=(pairs,),
        in_specs=[ispec] * 4
        + [pl.BlockSpec((128, tokens), lambda i: (i + place, 0))]
        + [pl.BlockSpec((1, 2, tokens), lambda i: (i + first, 0, 0))]
        + [const_spec(z.shape) for z in (cos, sin, aux_q, aux_k)],
        out_specs=[tspec] * 3,
        out_shape=[tshape] * 3,
        scratch_shapes=[pltpu.VMEM((HEAD_DIM, tokens), F32)],
        compiler_params=params(),
        cost_estimate=lasts(12 * pairs),
        name="attn_bwd",
    )(qt, kt, vt, ot, dobt, lse, cos, sin, aux_q, aux_k)


def token_kernel(sizes, dab, *refs):
    wq, wk, wv, out = refs[3 * sum(sizes) :]
    total = dab[...].astype(F32)
    at = 0
    for three in joined(refs, sizes):
        sl = slice(at, at + three[0].shape[0])
        at = sl.stop
        for d, w in zip(three, (wq, wk, wv)):
            total = total + lax.dot_general(
                d, w[:, sl], (((0,), (1,)), ((), ())), preferred_element_type=F32
            )
    out[...] = total.astype(BF)


def token_grad_pass(dab, units, wq, wk, wv, block=512):
    tokens, depth = dab.shape
    row = pl.BlockSpec((block, depth), lambda i: (i, 0))
    flat = [z for unit in units for z in unit]
    return pl.pallas_call(
        functools.partial(token_kernel, unit_sizes(units, depth // 3)),
        grid=(tokens // block,),
        in_specs=[row]
        + [pl.BlockSpec((z.shape[0], block), lambda i: (0, i)) for z in flat]
        + [const_spec(z.shape) for z in (wq, wk, wv)],
        out_specs=row,
        out_shape=jax.ShapeDtypeStruct((tokens, depth), BF),
        compiler_params=params(),
        cost_estimate=lasts(10),
        name="token_grad",
    )(dab, *flat, wq, wk, wv)


def join_halves(side, value, other, full):
    half = value.shape[1]
    full[:, pl.ds(pl.multiple_of(side * half, half), half)] = value[...].astype(F32)
    full[:, pl.ds(pl.multiple_of((1 - side) * half, half), half)] = other[...].astype(F32)


def finish_kernel(plan, count, side, *refs):
    ins, refs = refs[: 2 * count], refs[2 * count :]
    outs, full = refs[: len(plan)], refs[len(plan) :]
    for i in range(count):
        value, other = ins[2 * i], ins[2 * i + 1]
        if value.shape[1] < full[i].shape[1]:
            join_halves(side[0], value, other, full[i])
        else:
            full[i][...] = value[...].astype(F32) + other[...].astype(F32)
    for out, blocks in zip(outs, plan):
        for (i, row, column), (height, width), (to_row, to_column) in blocks:
            out[to_row : to_row + height, to_column : to_column + width] = full[i][
                row : row + height, column : column + width
            ]


def finish(side, pairs, depth, plan):
    sizes = []
    for blocks in plan:
        sizes.append(tuple(max(b[2][d] + b[1][d] for b in blocks) for d in range(2)))
    flat = [z for pair in pairs for z in pair]
    return pl.pallas_call(
        functools.partial(finish_kernel, plan, len(pairs)),
        grid_spec=pltpu.PrefetchScalarGridSpec(
            num_scalar_prefetch=1,
            grid=(1,),
            in_specs=[const_spec(z.shape) for z in flat],
            out_specs=[const_spec(z) for z in sizes],
            scratch_shapes=[pltpu.VMEM((pair[0].shape[0], depth), F32) for pair in pairs],
        ),
        out_shape=[jax.ShapeDtypeStruct(z, F32) for z in sizes],
        compiler_params=params(),
        cost_estimate=lasts(3),
        name="finish",
    )(side, *flat)


def swap(z, axis, bit):
    size = lax.axis_size(axis)
    return lax.ppermute(z, axis, [(i, i ^ bit) for i in range(size)])


def bits_of(size):
    return [1 << k for k in range(size.bit_length() - 1)]


def after(values, *deps):
    return lax.optimization_barrier((values, deps))[0]


def far_pieces(z):
    held = {0: z}
    for bit in reversed(bits_of(lax.axis_size("fsdp"))[1:]):
        held.update({j | bit: swap(piece, "fsdp", bit) for j, piece in list(held.items())})
    return held


def near_pieces(held):
    held = dict(held)
    held.update({j | 1: swap(piece, "fsdp", 1) for j, piece in list(held.items())})
    return [held[j] for j in range(len(held))]


def own_order(z, me):
    for bit in bits_of(z.shape[0]):
        flipped = z.reshape(-1, 2, bit, *z.shape[1:])[:, ::-1].reshape(z.shape)
        z = jnp.where((me & bit) == 0, z, flipped)
    return z


def total(terms):
    out = terms[0].astype(F32)
    for term in terms[1:]:
        out = out + term.astype(F32)
    return out


class Sums:
    def __init__(self):
        self.sent = []

    def swap(self, z, axis, bit):
        self.sent.append(z)
        return swap(z, axis, bit)

    def near(self, parts):
        terms = {j: [part] for j, part in enumerate(parts)}
        for j in [j for j in terms if j & 1]:
            terms[j ^ 1].append(self.swap(terms.pop(j)[0], "fsdp", 1))
        return terms

    def far(self, terms):
        terms = dict(terms)
        for bit in bits_of(lax.axis_size("fsdp"))[1:]:
            for j in [j for j in terms if j & bit]:
                value = total(terms.pop(j)).astype(BF)
                terms[j ^ bit] = terms[j ^ bit] + [self.swap(value, "fsdp", bit)]
        return terms[0]

    def halves(self, terms):
        half = terms[0].shape[1] // 2
        side = lax.axis_index("dp") % 2
        away = [lax.dynamic_slice_in_dim(t, (1 - side) * half, half, 1) for t in terms]
        here = [lax.dynamic_slice_in_dim(t, side * half, half, 1) for t in terms]
        return here + [self.swap(total(away).astype(BF), "dp", 1)]

    def pair_up(self, terms, bit):
        value = total(terms).astype(BF)
        return [value, self.swap(value, "dp", bit)]


def shards(
    tokens, cotangent, bucket, key_lengths,
    query_weight, key_weight, value_weight, output_weight, up_weight, down_weight,
    query_bias, key_bias, value_bias, output_bias, up_bias, down_bias,
    first_gain, first_shift, second_gain, second_shift,
):
    count = lax.axis_size("fsdp")
    me_scalar = lax.axis_index("fsdp").astype(jnp.int32)
    me = me_scalar[None]
    row_count, depth = tokens.shape
    rows = depth // count
    wide_rows = up_bias.shape[0]

    dp_size = lax.axis_size("dp")
    side = (lax.axis_index("dp") % 2).astype(jnp.int32)[None]
    pairs = depth // 128
    cut = pairs // 3
    qkv1, qkv2 = pack(query_weight, key_weight, value_weight, cut * 128)
    names = (
        query_bias, key_bias, value_bias, output_bias, down_bias,
        first_gain, first_shift, second_gain, second_shift, up_bias,
    )
    names = after(names, qkv1)
    narrow = jnp.stack([jnp.pad(z, (0, wide_rows - rows)) for z in names[:9]] + [names[9]])
    narrow = jnp.pad(narrow, ((0, 6), (0, 0)))
    qkv1 = far_pieces(qkv1)
    qkv2 = far_pieces(qkv2)
    thin = near_pieces(far_pieces(narrow))
    up_here, up_away = split(side, after(up_weight, narrow))
    aux_q, aux_k, cos, sin = layout_tables(after(bucket, up_here)[0], key_lengths[0], row_count)
    xt = after(tokens, up_here).T
    qkv1 = near_pieces(after(qkv1, xt, aux_q, aux_k, cos, sin))
    up_here = after(up_here, list(qkv1))
    wu_here = far_pieces(up_here)

    thin = own_order(jnp.stack(thin), me_scalar).astype(F32)
    vectors = thin[:, :9, :rows].transpose(1, 0, 2).reshape(9, depth)
    bu = thin[:, 9].reshape(1, -1)
    bias3 = vectors[:3].T
    vec = jnp.pad(vectors[3:], ((0, 2), (0, 0)))

    tables = (cos, sin, aux_q, aux_k)
    bias2 = bias3[cut * 128 :]
    fwd = [attn_fwd(me, 0, cut, xt, qkv1, bias3[: cut * 128], *tables)]
    qkv2 = near_pieces(after(qkv2, fwd[0][0]))
    out_w, down_w = after((output_weight, down_weight), list(qkv2))
    wo = far_pieces(out_w)
    wd = far_pieces(down_w)
    fwd.append(attn_fwd(me, 0, cut, after(xt, out_w, down_w), qkv2, bias2, *tables))
    wu_here = after(wu_here, fwd[1][0])
    wu_away = {0: up_away}
    wu_away.update({j: swap(z, "dp", 1) for j, z in wu_here.items() if j})
    fwd.append(
        attn_fwd(me, cut, cut, after(xt, list(wu_here.values())), qkv2, bias2, *tables)
    )
    wo, wd, wu_away = after((wo, wd, wu_away), fwd[2][0])
    wu_here, wo, wd, wu_away = (near_pieces(z) for z in (wu_here, wo, wd, wu_away))
    ot = jnp.concatenate([z[3] for z in fwd], axis=0)
    wq, wk, wv = (jnp.concatenate([z[i] for z in fwd], axis=1) for i in (5, 6, 7))
    who = jnp.concatenate([me, side])
    y, gb, dub, h1b, dfb, dab, dobt, small, dbu = rows_pass(
        who, tokens, ot, cotangent, wo, wu_here + wu_away, wd, vec, bu
    )

    sums = Sums()
    done = []

    def then(terms):
        return after(terms, done)

    u_parts = up_grads(me, h1b, dub, count)
    u_terms = sums.near(u_parts)
    d_parts = down_out_grads(me, after(gb, u_parts), dfb, ot, dab, small, dbu, count)
    done[:] = [d_parts[0]]
    u_terms = sums.far(then(u_terms))
    d_terms = sums.near(d_parts)

    rest = bits_of(dp_size)[1:]
    lines = [list(range(i, dp_size, 2)) for i in range(2)]

    def backward(i, many):
        part = fwd[i // cut]
        args = after((*part[:4], dobt), sums.sent, done)
        out = attn_bwd(i % cut, many, i, *args, part[4], cos, sin, aux_q, aux_k)
        done[:] = [out[0]]
        return out

    def units(outs):
        args = after(outs, sums.sent)
        parts = qkv_grads(me, xt, args, count)
        done[:] = [parts[0]]
        return parts

    def line_sum(terms, noted):
        value = total(terms).astype(BF)
        if noted:
            sums.sent.append(value)
        return lax.psum(value, "dp", axis_index_groups=lines)

    def other_half(value):
        return (value, sums.swap(value, "dp", 1))

    tiles = up_weight.shape[1] // depth
    back = [backward(0, 2)]
    u_terms = sums.halves(then(u_terms))
    d_terms = sums.far(then(d_terms))
    back.append(backward(2, 1))
    u_value = line_sum(then(u_terms), True)
    back.append(backward(3, 1))
    d_terms = sums.halves(then(d_terms))
    a_terms = sums.near(units(back))
    back.append(backward(4, 1))
    a_terms = sums.far(then(a_terms))
    d_value = line_sum(after(d_terms, done, u_value), False)
    done.append(u_value)
    back.append(backward(5, 1))
    a_terms = sums.halves(then(a_terms))
    u_pair = other_half(then(u_value))
    c_terms = sums.near(units(back[3:]))
    a_terms = sums.pair_up(then(a_terms), rest[0])
    c_terms = sums.far(then(c_terms))
    dab = after(dab, sums.sent, done)
    token_grad = token_grad_pass(dab, back, wq, wk, wv)
    done[:] = [token_grad]
    c_terms = sums.pair_up(then(c_terms), 1)
    for bit in rest[1:]:
        a_terms = sums.pair_up(then(a_terms), bit)
    (d_up,) = finish(
        side, [after(u_pair, sums.sent, done)], depth,
        [[((0, t * rows, 0), (rows, depth), (0, t * depth)) for t in range(tiles)]],
    )
    done[:] = [d_up]
    d_pair = other_half(then(d_value))
    for bit in rest:
        c_terms = sums.pair_up(c_terms, bit)
    a_pair = other_half(total(a_terms).astype(BF))

    height = down_weight.shape[0]
    unit = depth // 3
    place = [(0, 0), (0, rows), (1, 0)]
    d_down, d_out, thin = finish(
        side, [d_pair], depth,
        [
            [((0, 0, 0), (height, depth), (0, 0))],
            [((0, height, 0), (rows, depth), (0, 0))],
            [((0, height + rows, 0), (16, depth), (0, 0))],
        ],
    )
    d_q, d_k, d_v, bias = finish(
        side, [a_pair, c_terms], depth,
        [
            [((i, row, t * unit), (rows, unit), (0, u * unit)) for u, (i, row) in enumerate(place)]
            for t in range(3)
        ]
        + [[((0, 2 * rows, 0), (16, depth), (0, 0)), ((1, rows, 0), (16, depth), (16, 0))]],
    )

    def own(z):
        return lax.dynamic_slice_in_dim(z, me_scalar * rows, rows, z.ndim - 1)

    b_o, b_d, gain1, shift1, gain2, shift2 = own(thin[:6])
    b_up = lax.dynamic_slice_in_dim(thin[8 : 8 + tiles].reshape(-1), me_scalar * wide_rows, wide_rows, 0)
    bias = jnp.stack([bias[0], bias[1], bias[16]]).reshape(3, 3, unit).transpose(1, 0, 2)
    b_q, b_k, b_v = own(bias.reshape(3, depth))
    return (
        y, token_grad, d_q, d_k, d_v, d_out, d_up, d_down,
        b_q, b_k, b_v, b_o, b_up, b_d, gain1, shift1, gain2, shift2,
    )


def solution(mesh):
    rows = P(("dp", "fsdp"), None)
    mat = P("fsdp", None)
    vector = P("fsdp")
    in_specs = (rows, rows, P(("dp", "fsdp")), rows) + (mat,) * 6 + (vector,) * 10
    out_specs = (rows, rows) + (mat,) * 6 + (vector,) * 10
    return jax.shard_map(shards, mesh=mesh, in_specs=in_specs, out_specs=out_specs, check_vma=False)
```

```python
import functools

import jax
import jax.numpy as jnp
from jax import lax
from jax.experimental import pallas as pl
from jax.experimental.pallas import tpu as pltpu
from jax.sharding import PartitionSpec as P

HEAD_DIM = 64
HALF = 32
SLOT = 512
AUX = 16
NEG = -1e30
LOG2E = 1.4426950408889634
LN2 = 0.6931471805599453
QSCALE = 0.125 * LOG2E
BF = jnp.bfloat16
F32 = jnp.float32
NN = ((1,), (0,))
NT = ((1,), (1,))
TN = ((0,), (0,))
ERFC_P = 0.37
ERFC_C = (
    0.20835304049472436,
    0.2152118908535975,
    0.15105251587527643,
    0.3213824037594925,
    -0.19174412290346565,
    0.4392956874015427,
    -0.14355086909593573,
)
VMEM_LIMIT = 60 << 20


def lasts(us):
    return pl.CostEstimate(flops=us * 1000000000, bytes_accessed=us * 3000000, transcendentals=0)


def dot(a, b, dims=NN):
    return lax.dot_general(a, b, (dims, ((), ())), preferred_element_type=F32)


def params(**kw):
    return pltpu.CompilerParams(vmem_limit_bytes=VMEM_LIMIT, **kw)


def const_spec(shape):
    return pl.BlockSpec(shape, lambda *_: (0,) * len(shape), pipeline_mode=pl.Buffered(1))


def layout_tables(bucket_value, lengths_row, row_count):
    places = jnp.arange(row_count, dtype=jnp.int32)
    slot_index = places // SLOT
    sequence = jnp.where(
        bucket_value == 0, slot_index, jnp.where(bucket_value == 1, slot_index // 2, 0)
    )
    starts = jnp.where(
        bucket_value == 0,
        slot_index * SLOT,
        jnp.where(bucket_value == 1, slot_index // 2 * 2 * SLOT, 0),
    )
    offsets = places - starts
    limits = jnp.zeros_like(places)
    for member in range(3):
        limits = limits + jnp.where(sequence == member, lengths_row[member], 0)
    valid = offsets < limits
    rows = jnp.arange(AUX, dtype=jnp.int32)[:, None]
    same = (rows == sequence[None, :]) & (rows < 3)
    aux_q = jnp.where(same, 1.0, 0.0).astype(BF)
    aux_k = jnp.where(
        rows < 3,
        jnp.where(same & valid[None, :], 0.0, NEG),
        jnp.where(rows < 6, 1.0, 0.0),
    ).astype(BF)
    exponents = jnp.arange(HALF, dtype=F32) * (-2.0 / HEAD_DIM)
    inverse = jnp.power(jnp.float32(10000.0), exponents)
    angles = inverse[:, None] * offsets.astype(F32)[None, :]
    return aux_q, aux_k, jnp.cos(angles), jnp.sin(angles)


def turn(z, cos, sin):
    a, b = z[:HALF], z[HALF:]
    return jnp.concatenate([a * cos - b * sin, b * cos + a * sin], axis=0)


def pack_kernel(cut, wq, wk, wv, one, two):
    depth = wq.shape[1]
    for t, w in enumerate((wq, wk, wv)):
        one[:, t * cut : (t + 1) * cut] = w[:, :cut]
        two[:, t * (depth - cut) : (t + 1) * (depth - cut)] = w[:, cut:]


def pack(wq, wk, wv, cut):
    rows, depth = wq.shape
    sizes = [(rows, 3 * cut), (rows, 3 * (depth - cut))]
    return pl.pallas_call(
        functools.partial(pack_kernel, cut),
        grid=(1,),
        in_specs=[const_spec(wq.shape)] * 3,
        out_specs=[const_spec(z) for z in sizes],
        out_shape=[jax.ShapeDtypeStruct(z, BF) for z in sizes],
        compiler_params=params(),
        cost_estimate=lasts(2),
        name="pack",
    )(wq, wk, wv)


def split_kernel(side, w, here, away):
    half = here.shape[1]
    here[...] = w[:, pl.ds(pl.multiple_of(side[0] * half, half), half)]
    away[...] = w[:, pl.ds(pl.multiple_of((1 - side[0]) * half, half), half)]


def split(side, w):
    rows, wide = w.shape
    size = (rows, wide // 2)
    return pl.pallas_call(
        split_kernel,
        grid_spec=pltpu.PrefetchScalarGridSpec(
            num_scalar_prefetch=1,
            grid=(1,),
            in_specs=[const_spec(w.shape)],
            out_specs=[const_spec(size)] * 2,
        ),
        out_shape=[jax.ShapeDtypeStruct(size, BF)] * 2,
        compiler_params=params(),
        cost_estimate=lasts(2),
        name="split",
    )(side, w)


def attn_fwd_kernel(chunk, count, me, xt, *refs):
    pieces_in, refs = refs[: 3 * count], refs[3 * count :]
    bias, cos, sin, aux_q, aux_k, qt, kt, vt, ot, lse, wq, wk, wv, acc, top = refs
    tokens = xt.shape[1]
    x = xt[...]
    for col, (w, out) in enumerate(((wq, qt), (wk, kt), (wv, vt))):
        for j in range(count):
            piece = pieces_in[col * count + j]
            rows = piece.shape[0]
            w[pl.ds(pl.multiple_of((me[0] ^ j) * rows, rows), rows), :] = piece[...]
        z = dot(w[...], x, TN) + bias[:, col : col + 1]
        if col == 2:
            out[...] = z.astype(BF)
            continue
        for h in range(2):
            r = turn(z[h * HEAD_DIM : (h + 1) * HEAD_DIM], cos[...], sin[...])
            if col == 0:
                r = r * QSCALE
            out[h * HEAD_DIM : (h + 1) * HEAD_DIM, :] = r.astype(BF)
    ones = jnp.ones((AUX, tokens), BF)
    for h in range(2):
        rows = slice(h * HEAD_DIM, (h + 1) * HEAD_DIM)
        q32 = qt[rows, :].astype(F32)
        k32 = kt[rows, :].astype(F32)
        bound = jnp.max(jnp.sum(q32 * q32, axis=0)) * jnp.max(jnp.sum(k32 * k32, axis=0))
        qa = jnp.concatenate([qt[rows, :], aux_q[...]], axis=0)
        ka = jnp.concatenate([kt[rows, :], aux_k[...]], axis=0).T
        va = jnp.concatenate([vt[rows, :], ones], axis=0)
        small = bound < 8100.0

        @pl.when(small)
        def _():
            total = None
            for c in range(tokens // chunk):
                sl = slice(c * chunk, (c + 1) * chunk)
                p = jnp.exp2(dot(ka[sl], qa)).astype(BF)
                part = dot(va[:, sl], p)
                total = part if total is None else total + part
            acc[...] = total
            top[...] = jnp.zeros_like(top)

        @pl.when(jnp.logical_not(small))
        def _():
            total = None
            for c in range(tokens // chunk):
                sl = slice(c * chunk, (c + 1) * chunk)
                s = dot(ka[sl], qa)
                here = jnp.max(s, axis=0, keepdims=True)
                if c == 0:
                    best = here
                    total = dot(va[:, sl], jnp.exp2(s - best).astype(BF))
                else:
                    later = jnp.maximum(best, here)
                    part = dot(va[:, sl], jnp.exp2(s - later).astype(BF))
                    total = total * jnp.exp2(best - later) + part
                    best = later
            acc[...] = total
            top[...] = best

        row_total = acc[HEAD_DIM : HEAD_DIM + 1, :]
        ot[rows, :] = (acc[:HEAD_DIM, :] / row_total).astype(BF)
        lse[0, h : h + 1, :] = top[...] + jnp.log2(row_total)


def attn_fwd(me, first, pairs, xt, pieces_in, bias, cos, sin, aux_q, aux_k, chunk=512):
    depth, tokens = xt.shape
    count = len(pieces_in)
    rows = depth // count
    total_pairs = pieces_in[0].shape[1] // 384
    width = pairs * 128
    tspec = pl.BlockSpec((128, tokens), lambda i, me: (i, 0))
    tshape = jax.ShapeDtypeStruct((width, tokens), BF)
    piece_specs = [
        pl.BlockSpec((rows, 128), lambda i, me, col=col: (0, first + i + col * total_pairs))
        for col in range(3)
        for _ in range(count)
    ]
    wspec = pl.BlockSpec((depth, 128), lambda i, me: (0, i))
    return pl.pallas_call(
        functools.partial(attn_fwd_kernel, chunk, count),
        grid_spec=pltpu.PrefetchScalarGridSpec(
            num_scalar_prefetch=1,
            grid=(pairs,),
            in_specs=[const_spec(xt.shape)]
            + piece_specs
            + [pl.BlockSpec((128, 3), lambda i, me: (first + i, 0))]
            + [const_spec(z.shape) for z in (cos, sin, aux_q, aux_k)],
            out_specs=[tspec] * 4
            + [pl.BlockSpec((1, 2, tokens), lambda i, me: (i, 0, 0))]
            + [wspec] * 3,
            scratch_shapes=[
                pltpu.VMEM((HEAD_DIM + AUX, tokens), F32),
                pltpu.VMEM((1, tokens), F32),
            ],
        ),
        out_shape=[tshape] * 4
        + [jax.ShapeDtypeStruct((pairs, 2, tokens), F32)]
        + [jax.ShapeDtypeStruct((depth, width), BF)] * 3,
        compiler_params=params(),
        cost_estimate=lasts(7 * pairs),
        name="attn_fwd",
    )(me, xt, *(list(pieces_in) * 3), bias, cos, sin, aux_q, aux_k)


def norm_stats(r):
    center = r - jnp.mean(r, axis=-1, keepdims=True)
    rstd = lax.rsqrt(jnp.mean(center * center, axis=-1, keepdims=True) + 1e-5)
    return center * rstd, rstd


def norm_back(dyg, xhat, rstd):
    return rstd * (
        dyg
        - jnp.mean(dyg, axis=-1, keepdims=True)
        - xhat * jnp.mean(dyg * xhat, axis=-1, keepdims=True)
    )


def pl_reciprocal(d):
    return pltpu.reciprocal(d, approx=True)


def gelu_parts(u):
    e = jnp.exp2(u * u * (-0.5 * LOG2E))
    d = 1.0 + jnp.abs(u) * (ERFC_P * 0.7071067811865476)
    t = pl_reciprocal(d)
    t = t * (2.0 - d * t)
    poly = jnp.full_like(u, 0.5 * ERFC_C[-1])
    for coef in ERFC_C[-2::-1]:
        poly = poly * t + 0.5 * coef
    tail = poly * t * e
    phi_cum = jnp.where(u < 0, tail, 1.0 - tail)
    return u * phi_cum, phi_cum + u * (e * 0.3989422804014327)


def colsum(z):
    return jnp.sum(z, axis=0, keepdims=True)


def rows_kernel(count, me, x, ot, cot, vec, bu, *refs):
    pieces_in, refs = refs[: 4 * count], refs[4 * count :]
    y, gb_ref, dub_ref, h1b_ref, dfb_ref, dab_ref, dobt, small, dbu, wo, wu, wd, sems = refs

    wo, wu, wd = (w.reshape(w.shape[0] * 8, w.shape[2]) for w in (wo, wu, wd))
    half = wu.shape[1] // 2
    copies = []
    for col, w in enumerate((wo, wu, wu, wd)):
        for j in range(count):
            piece = pieces_in[col * count + j]
            rows = piece.shape[0]
            spot = pl.ds(pl.multiple_of((me[0] ^ j) * rows, rows), rows)
            if w is wu:
                at = pl.multiple_of((me[1] ^ (col - 1)) * half, half)
                place = w.at[spot, pl.ds(at, half)]
            else:
                place = w.at[spot, :]
            copies.append(pltpu.make_async_copy(piece, place, sems.at[col, j]))

    @pl.when(pl.program_id(0) == 0)
    def _():
        for copy in copies:
            copy.start()

    def arrived(first, last):
        @pl.when(pl.program_id(0) == 0)
        def _():
            for copy in copies[first * count : last * count]:
                copy.wait()

    arrived(0, 1)
    bo, bd = vec[0:1, :], vec[1:2, :]
    g1, c1, g2, c2 = vec[2:3, :], vec[3:4, :], vec[4:5, :], vec[5:6, :]
    a = dot(ot[...], wo[...], TN) + bo
    xhat1, rstd1 = norm_stats(x[...].astype(F32) + a)
    h1 = xhat1 * g1 + c1
    h1b = h1.astype(BF)
    h1b_ref[...] = h1b
    arrived(1, 3)
    u = dot(h1b, wu[...]) + bu[...]
    g, slope = gelu_parts(u)
    gb = g.astype(BF)
    gb_ref[...] = gb
    arrived(3, 4)
    f = dot(gb, wd[...]) + bd
    xhat2, rstd2 = norm_stats(h1 + f)
    y[...] = (xhat2 * g2 + c2).astype(BF)
    dy = cot[...].astype(F32)
    dr2 = norm_back(dy * g2, xhat2, rstd2)
    dfb = dr2.astype(BF)
    dfb_ref[...] = dfb
    dub = (dot(dfb, wd[...], NT) * slope).astype(BF)
    dub_ref[...] = dub
    dh1 = dr2 + dot(dub, wu[...], NT)
    dr1 = norm_back(dh1 * g1, xhat1, rstd1)
    dab = dr1.astype(BF)
    dab_ref[...] = dab
    dobt[...] = dot(wo[...], dab, NT).astype(BF)
    part = jnp.concatenate(
        [
            colsum(dab.astype(F32)),
            colsum(dfb.astype(F32)),
            colsum(dh1 * xhat1),
            colsum(dh1),
            colsum(dy * xhat2),
            colsum(dy),
            jnp.zeros((2, dy.shape[1]), F32),
        ],
        axis=0,
    )
    dbu_part = colsum(dub.astype(F32))

    @pl.when(pl.program_id(0) == 0)
    def _():
        small[...] = part
        dbu[...] = dbu_part

    @pl.when(pl.program_id(0) > 0)
    def _():
        small[...] += part
        dbu[...] += dbu_part


def rows_pass(me, x, ot, cot, wo, wu, wd, vec, bu, block=512):
    tokens, depth = x.shape
    wide = wu[0].shape[1] * 2
    count = len(wo)
    assert len(wu) == 2 * count
    row = pl.BlockSpec((block, depth), lambda i, me: (i, 0))
    row_wide = pl.BlockSpec((block, wide), lambda i, me: (i, 0))
    col = pl.BlockSpec((depth, block), lambda i, me: (0, i))
    narrow = jax.ShapeDtypeStruct((tokens, depth), BF)
    broad = jax.ShapeDtypeStruct((tokens, wide), BF)
    return pl.pallas_call(
        functools.partial(rows_kernel, count),
        grid_spec=pltpu.PrefetchScalarGridSpec(
            num_scalar_prefetch=1,
            grid=(tokens // block,),
            in_specs=[row, col, row]
            + [const_spec(z.shape) for z in (vec, bu)]
            + [pl.BlockSpec(memory_space=pl.ANY)] * (4 * count),
            out_specs=[row, row_wide, row_wide, row, row, row, col]
            + [const_spec((8, depth)), const_spec((1, wide))],
            scratch_shapes=[
                pltpu.VMEM((depth // 8, 8, depth), BF),
                pltpu.VMEM((depth // 8, 8, wide), BF),
                pltpu.VMEM((wide // 8, 8, depth), BF),
                pltpu.SemaphoreType.DMA((4, count)),
            ],
        ),
        out_shape=[
            narrow, broad, broad, narrow, narrow, narrow,
            jax.ShapeDtypeStruct((depth, tokens), BF),
            jax.ShapeDtypeStruct((8, depth), F32),
            jax.ShapeDtypeStruct((1, wide), F32),
        ],
        compiler_params=params(),
        cost_estimate=lasts(68),
        name="rows_pass",
    )(me, x, ot, cot, vec, bu, *wo, *wu, *wd)


def up_kernel(count, rows, me, h1b, dub, *refs):
    outs, result = refs[:count], refs[count]
    result[...] = dot(h1b[...], dub[...], TN)
    for j in range(count):
        spot = pl.ds(pl.multiple_of((me[0] ^ j) * rows, rows), rows)
        outs[j][...] = result[spot, :].astype(BF)


def up_grads(me, h1b, dub, count):
    tokens, depth = h1b.shape
    tiles = dub.shape[1] // depth
    rows = depth // count
    return pl.pallas_call(
        functools.partial(up_kernel, count, rows),
        grid_spec=pltpu.PrefetchScalarGridSpec(
            num_scalar_prefetch=1,
            grid=(tiles,),
            in_specs=[const_spec(h1b.shape), pl.BlockSpec((tokens, depth), lambda s, me: (0, s))],
            out_specs=[pl.BlockSpec((rows, depth), lambda s, me: (s, 0))] * count,
            scratch_shapes=[pltpu.VMEM((depth, depth), F32)],
        ),
        out_shape=[jax.ShapeDtypeStruct((tiles * rows, depth), BF)] * count,
        compiler_params=params(),
        cost_estimate=lasts(12),
        name="up_grads",
    )(me, h1b, dub)


def down_kernel(count, tiles, step_rows, me, gb, dfb, ot, dab, small, dbu, *refs):
    outs, result = refs[:count], refs[count]
    s = pl.program_id(0)
    height, depth = step_rows // count * tiles, dfb.shape[1]
    rows = depth // count

    @pl.when(s < tiles)
    def _():
        result[...] = dot(gb[...], dfb[...], TN)

    for t in range(tiles):
        per = step_rows // height if step_rows > height else 1

        @pl.when(s == t)
        def _():
            if per == 1:
                owner = t * step_rows // height
                at = t * step_rows % height
                for j in range(count):

                    @pl.when((me[0] ^ j) == owner)
                    def _():
                        outs[j][at : at + step_rows, :] = result[...].astype(BF)
            else:
                for i in range(per):
                    for j in range(count):

                        @pl.when((me[0] ^ j) == t * per + i)
                        def _():
                            part = result[i * height : (i + 1) * height, :]
                            outs[j][:height, :] = part.astype(BF)

    @pl.when(s == tiles)
    def _():
        result[...] = dot(ot[...], dab[...])
        wide = dbu.shape[1] // depth
        pad = jnp.zeros((16 - small.shape[0] - wide, depth), F32)
        lines = [small[...]] + [dbu[:, i * depth : (i + 1) * depth] for i in range(wide)] + [pad]
        lines = jnp.concatenate(lines, axis=0).astype(BF)
        for j in range(count):
            spot = pl.ds(pl.multiple_of((me[0] ^ j) * rows, rows), rows)
            outs[j][height : height + rows, :] = result[spot, :].astype(BF)
            outs[j][height + rows :, :] = lines


def down_out_grads(me, gb, dfb, ot, dab, small, dbu, count):
    tokens, wide = gb.shape
    depth = dfb.shape[1]
    tiles = wide // depth
    height = wide // count + depth // count + 16
    return pl.pallas_call(
        functools.partial(down_kernel, count, tiles, depth),
        grid_spec=pltpu.PrefetchScalarGridSpec(
            num_scalar_prefetch=1,
            grid=(tiles + 1,),
            in_specs=[pl.BlockSpec((tokens, depth), lambda s, me: (0, jnp.minimum(s, tiles - 1)))]
            + [const_spec(z.shape) for z in (dfb, ot, dab, small, dbu)],
            out_specs=[const_spec((height, depth))] * count,
            scratch_shapes=[pltpu.VMEM((depth, depth), F32)],
        ),
        out_shape=[jax.ShapeDtypeStruct((height, depth), BF)] * count,
        compiler_params=params(),
        cost_estimate=lasts(17),
        name="down_out_grads",
    )(me, gb, dfb, ot, dab, small, dbu)


def joined(refs, sizes):
    units, at = [], 0
    for size in sizes:
        threes = [refs[3 * (at + i) : 3 * (at + i) + 3] for i in range(size)]
        units.append([jnp.concatenate([z[t][...] for z in threes], axis=0) for t in range(3)])
        at += size
    return units


def unit_sizes(triples, unit):
    sizes, width = [], unit
    for three in triples:
        if width == unit:
            sizes.append(0)
            width = 0
        sizes[-1] += 1
        width += three[0].shape[0]
    return tuple(sizes)


def qkv_kernel(count, rows, sizes, me, xt, *refs):
    ins, outs, result = refs[: 3 * sum(sizes)], refs[3 * sum(sizes) : -1], refs[-1]
    units = len(sizes)
    unit = xt.shape[0] // 3
    ones = jnp.ones((16, xt.shape[1]), BF)
    line = lax.broadcasted_iota(jnp.int32, (16, 1), 0)
    arrays = joined(ins, sizes)
    for t in range(3):
        columns = slice(t * unit, (t + 1) * unit)
        bias = jnp.zeros((16, unit), F32)
        for u in range(units):
            d = arrays[u][t]
            result[...] = dot(xt[...], d, NT)
            bias = bias + jnp.where(line == u, dot(ones, d, NT), 0.0)
            for j in range(count):
                spot = pl.ds(pl.multiple_of((me[0] ^ j) * rows, rows), rows)
                outs[j][u * rows : (u + 1) * rows, columns] = result[spot, :].astype(BF)
        for j in range(count):
            outs[j][units * rows :, columns] = bias.astype(BF)


def qkv_grads(me, xt, triples, count):
    depth, tokens = xt.shape
    unit = depth // 3
    sizes = unit_sizes(triples, unit)
    units = len(sizes)
    flat = [z for three in triples for z in three]
    rows = depth // count
    shape = (units * rows + 16, depth)
    return pl.pallas_call(
        functools.partial(qkv_kernel, count, rows, sizes),
        grid_spec=pltpu.PrefetchScalarGridSpec(
            num_scalar_prefetch=1,
            grid=(1,),
            in_specs=[const_spec(z.shape) for z in [xt] + flat],
            out_specs=[const_spec(shape)] * count,
            scratch_shapes=[pltpu.VMEM((depth, unit), F32)],
        ),
        out_shape=[jax.ShapeDtypeStruct(shape, BF)] * count,
        compiler_params=params(),
        cost_estimate=lasts(4 * units + 2),
        name="qkv_grads",
    )(me, xt, *flat)


def pieces(row):
    first = row.astype(BF)
    rest = row - first.astype(F32)
    second = rest.astype(BF)
    third = (rest - second.astype(F32)).astype(BF)
    return first.astype(F32), second.astype(F32), third.astype(F32)


def shift_rows(row, base):
    index = lax.broadcasted_iota(jnp.int32, (AUX, row.shape[1]), 0)
    out = base
    for i, piece in enumerate(pieces(row)):
        out = jnp.where(index == 3 + i, piece, out)
    return out.astype(BF)


def attn_bwd_kernel(chunk, qt, kt, vt, ot, dot_, lse, cos, sin, aux_q, aux_k, dqt, dkt, dvt, dq_acc):
    tokens = qt.shape[1]
    index = lax.broadcasted_iota(jnp.int32, (AUX, tokens), 0)
    aux_v = jnp.where((index >= 3) & (index < 6), 1.0, 0.0).astype(BF)
    for h in range(2):
        rows = slice(h * HEAD_DIM, (h + 1) * HEAD_DIM)
        q, k, v, do = qt[rows, :], kt[rows, :], vt[rows, :], dot_[rows, :]
        delta = jnp.sum(do.astype(F32) * ot[rows, :].astype(F32), axis=0, keepdims=True)
        qa = jnp.concatenate([q, shift_rows(-lse[0, h : h + 1, :], aux_q[...].astype(F32))], axis=0).T
        ka = jnp.concatenate([k, aux_k[...]], axis=0)
        da = jnp.concatenate([do, shift_rows(-delta, jnp.zeros((AUX, tokens), F32))], axis=0).T
        va = jnp.concatenate([v, aux_v], axis=0)
        dv = dk = None
        for c in range(tokens // chunk):
            sl = slice(c * chunk, (c + 1) * chunk)
            p = jnp.exp2(dot(qa[sl], ka))
            ds = (p * dot(da[sl], va)).astype(BF)
            dv_part = dot(do[:, sl], p.astype(BF))
            dk_part = dot(q[:, sl], ds)
            dv = dv_part if dv is None else dv + dv_part
            dk = dk_part if dk is None else dk + dk_part
            dq_acc[:, sl] = dot(k, ds, NT)
        dk = turn(dk * LN2, cos[...], -sin[...])
        dq = turn(dq_acc[...] * 0.125, cos[...], -sin[...])
        for out, value in ((dqt, dq), (dkt, dk), (dvt, dv)):
            out[rows, :] = value.astype(BF)


def attn_bwd(first, pairs, place, qt, kt, vt, ot, dobt, lse, cos, sin, aux_q, aux_k, chunk=256):
    tokens = qt.shape[1]
    ispec = pl.BlockSpec((128, tokens), lambda i: (i + first, 0))
    tspec = pl.BlockSpec((128, tokens), lambda i: (i, 0))
    tshape = jax.ShapeDtypeStruct((128 * pairs, tokens), BF)
    return pl.pallas_call(
        functools.partial(attn_bwd_kernel, chunk),
        grid=(pairs,),
        in_specs=[ispec] * 4
        + [pl.BlockSpec((128, tokens), lambda i: (i + place, 0))]
        + [pl.BlockSpec((1, 2, tokens), lambda i: (i + first, 0, 0))]
        + [const_spec(z.shape) for z in (cos, sin, aux_q, aux_k)],
        out_specs=[tspec] * 3,
        out_shape=[tshape] * 3,
        scratch_shapes=[pltpu.VMEM((HEAD_DIM, tokens), F32)],
        compiler_params=params(),
        cost_estimate=lasts(12 * pairs),
        name="attn_bwd",
    )(qt, kt, vt, ot, dobt, lse, cos, sin, aux_q, aux_k)


def token_kernel(sizes, dab, *refs):
    wq, wk, wv, out = refs[3 * sum(sizes) :]
    total = dab[...].astype(F32)
    at = 0
    for three in joined(refs, sizes):
        sl = slice(at, at + three[0].shape[0])
        at = sl.stop
        for d, w in zip(three, (wq, wk, wv)):
            total = total + lax.dot_general(
                d, w[:, sl], (((0,), (1,)), ((), ())), preferred_element_type=F32
            )
    out[...] = total.astype(BF)


def token_grad_pass(dab, units, wq, wk, wv, block=512):
    tokens, depth = dab.shape
    row = pl.BlockSpec((block, depth), lambda i: (i, 0))
    flat = [z for unit in units for z in unit]
    return pl.pallas_call(
        functools.partial(token_kernel, unit_sizes(units, depth // 3)),
        grid=(tokens // block,),
        in_specs=[row]
        + [pl.BlockSpec((z.shape[0], block), lambda i: (0, i)) for z in flat]
        + [const_spec(z.shape) for z in (wq, wk, wv)],
        out_specs=row,
        out_shape=jax.ShapeDtypeStruct((tokens, depth), BF),
        compiler_params=params(),
        cost_estimate=lasts(10),
        name="token_grad",
    )(dab, *flat, wq, wk, wv)


def join_halves(side, value, other, full):
    half = value.shape[1]
    full[:, pl.ds(pl.multiple_of(side * half, half), half)] = value[...].astype(F32)
    full[:, pl.ds(pl.multiple_of((1 - side) * half, half), half)] = other[...].astype(F32)


def finish_kernel(plan, count, side, *refs):
    ins, refs = refs[: 2 * count], refs[2 * count :]
    outs, full = refs[: len(plan)], refs[len(plan) :]
    for i in range(count):
        value, other = ins[2 * i], ins[2 * i + 1]
        if value.shape[1] < full[i].shape[1]:
            join_halves(side[0], value, other, full[i])
        else:
            full[i][...] = value[...].astype(F32) + other[...].astype(F32)
    for out, blocks in zip(outs, plan):
        for (i, row, column), (height, width), (to_row, to_column) in blocks:
            out[to_row : to_row + height, to_column : to_column + width] = full[i][
                row : row + height, column : column + width
            ]


def finish(side, pairs, depth, plan):
    sizes = []
    for blocks in plan:
        sizes.append(tuple(max(b[2][d] + b[1][d] for b in blocks) for d in range(2)))
    flat = [z for pair in pairs for z in pair]
    return pl.pallas_call(
        functools.partial(finish_kernel, plan, len(pairs)),
        grid_spec=pltpu.PrefetchScalarGridSpec(
            num_scalar_prefetch=1,
            grid=(1,),
            in_specs=[const_spec(z.shape) for z in flat],
            out_specs=[const_spec(z) for z in sizes],
            scratch_shapes=[pltpu.VMEM((pair[0].shape[0], depth), F32) for pair in pairs],
        ),
        out_shape=[jax.ShapeDtypeStruct(z, F32) for z in sizes],
        compiler_params=params(),
        cost_estimate=lasts(3),
        name="finish",
    )(side, *flat)


def swap(z, axis, bit):
    size = lax.axis_size(axis)
    return lax.ppermute(z, axis, [(i, i ^ bit) for i in range(size)])


def bits_of(size):
    return [1 << k for k in range(size.bit_length() - 1)]


def after(values, *deps):
    return lax.optimization_barrier((values, deps))[0]


def far_pieces(z):
    held = {0: z}
    for bit in reversed(bits_of(lax.axis_size("fsdp"))[1:]):
        held.update({j | bit: swap(piece, "fsdp", bit) for j, piece in list(held.items())})
    return held


def near_pieces(held):
    held = dict(held)
    held.update({j | 1: swap(piece, "fsdp", 1) for j, piece in list(held.items())})
    return [held[j] for j in range(len(held))]


def own_order(z, me):
    for bit in bits_of(z.shape[0]):
        flipped = z.reshape(-1, 2, bit, *z.shape[1:])[:, ::-1].reshape(z.shape)
        z = jnp.where((me & bit) == 0, z, flipped)
    return z


def total(terms):
    out = terms[0].astype(F32)
    for term in terms[1:]:
        out = out + term.astype(F32)
    return out


class Sums:
    def __init__(self):
        self.sent = []

    def swap(self, z, axis, bit):
        self.sent.append(z)
        return swap(z, axis, bit)

    def near(self, parts):
        terms = {j: [part] for j, part in enumerate(parts)}
        for j in [j for j in terms if j & 1]:
            terms[j ^ 1].append(self.swap(terms.pop(j)[0], "fsdp", 1))
        return terms

    def far(self, terms):
        terms = dict(terms)
        for bit in bits_of(lax.axis_size("fsdp"))[1:]:
            for j in [j for j in terms if j & bit]:
                value = total(terms.pop(j)).astype(BF)
                terms[j ^ bit] = terms[j ^ bit] + [self.swap(value, "fsdp", bit)]
        return terms[0]

    def halves(self, terms):
        half = terms[0].shape[1] // 2
        side = lax.axis_index("dp") % 2
        away = [lax.dynamic_slice_in_dim(t, (1 - side) * half, half, 1) for t in terms]
        here = [lax.dynamic_slice_in_dim(t, side * half, half, 1) for t in terms]
        return here + [self.swap(total(away).astype(BF), "dp", 1)]

    def pair_up(self, terms, bit):
        value = total(terms).astype(BF)
        return [value, self.swap(value, "dp", bit)]


def shards(
    tokens, cotangent, bucket, key_lengths,
    query_weight, key_weight, value_weight, output_weight, up_weight, down_weight,
    query_bias, key_bias, value_bias, output_bias, up_bias, down_bias,
    first_gain, first_shift, second_gain, second_shift,
):
    count = lax.axis_size("fsdp")
    me_scalar = lax.axis_index("fsdp").astype(jnp.int32)
    me = me_scalar[None]
    row_count, depth = tokens.shape
    rows = depth // count
    wide_rows = up_bias.shape[0]

    dp_size = lax.axis_size("dp")
    side = (lax.axis_index("dp") % 2).astype(jnp.int32)[None]
    pairs = depth // 128
    cut = pairs // 3
    qkv1, qkv2 = pack(query_weight, key_weight, value_weight, cut * 128)
    names = (
        query_bias, key_bias, value_bias, output_bias, down_bias,
        first_gain, first_shift, second_gain, second_shift, up_bias,
    )
    names = after(names, qkv1)
    narrow = jnp.stack([jnp.pad(z, (0, wide_rows - rows)) for z in names[:9]] + [names[9]])
    narrow = jnp.pad(narrow, ((0, 6), (0, 0)))
    qkv1 = far_pieces(qkv1)
    qkv2 = far_pieces(qkv2)
    thin = near_pieces(far_pieces(narrow))
    up_here, up_away = split(side, after(up_weight, narrow))
    aux_q, aux_k, cos, sin = layout_tables(after(bucket, up_here)[0], key_lengths[0], row_count)
    xt = after(tokens, up_here).T
    qkv1 = near_pieces(after(qkv1, xt, aux_q, aux_k, cos, sin))
    up_here = after(up_here, list(qkv1))
    wu_here = far_pieces(up_here)

    thin = own_order(jnp.stack(thin), me_scalar).astype(F32)
    vectors = thin[:, :9, :rows].transpose(1, 0, 2).reshape(9, depth)
    bu = thin[:, 9].reshape(1, -1)
    bias3 = vectors[:3].T
    vec = jnp.pad(vectors[3:], ((0, 2), (0, 0)))

    tables = (cos, sin, aux_q, aux_k)
    bias2 = bias3[cut * 128 :]
    fwd = [attn_fwd(me, 0, cut, xt, qkv1, bias3[: cut * 128], *tables)]
    qkv2 = near_pieces(after(qkv2, fwd[0][0]))
    out_w, down_w = after((output_weight, down_weight), list(qkv2))
    wo = far_pieces(out_w)
    wd = far_pieces(down_w)
    fwd.append(attn_fwd(me, 0, cut, after(xt, out_w, down_w), qkv2, bias2, *tables))
    wu_here = after(wu_here, fwd[1][0])
    wu_away = {0: up_away}
    wu_away.update({j: swap(z, "dp", 1) for j, z in wu_here.items() if j})
    fwd.append(
        attn_fwd(me, cut, cut, after(xt, list(wu_here.values())), qkv2, bias2, *tables)
    )
    wo, wd, wu_away = after((wo, wd, wu_away), fwd[2][0])
    wu_here, wo, wd, wu_away = (near_pieces(z) for z in (wu_here, wo, wd, wu_away))
    ot = jnp.concatenate([z[3] for z in fwd], axis=0)
    wq, wk, wv = (jnp.concatenate([z[i] for z in fwd], axis=1) for i in (5, 6, 7))
    who = jnp.concatenate([me, side])
    y, gb, dub, h1b, dfb, dab, dobt, small, dbu = rows_pass(
        who, tokens, ot, cotangent, wo, wu_here + wu_away, wd, vec, bu
    )

    sums = Sums()
    done = []

    def then(terms):
        return after(terms, done)

    u_parts = up_grads(me, h1b, dub, count)
    u_terms = sums.near(u_parts)
    d_parts = down_out_grads(me, after(gb, u_parts), dfb, ot, dab, small, dbu, count)
    done[:] = [d_parts[0]]
    u_terms = sums.far(then(u_terms))
    d_terms = sums.near(d_parts)

    rest = bits_of(dp_size)[1:]
    lines = [list(range(i, dp_size, 2)) for i in range(2)]

    def backward(i, many):
        part = fwd[i // cut]
        args = after((*part[:4], dobt), sums.sent, done)
        out = attn_bwd(i % cut, many, i, *args, part[4], cos, sin, aux_q, aux_k)
        done[:] = [out[0]]
        return out

    def units(outs):
        args = after(outs, sums.sent)
        parts = qkv_grads(me, xt, args, count)
        done[:] = [parts[0]]
        return parts

    def line_sum(terms, noted):
        value = total(terms).astype(BF)
        if noted:
            sums.sent.append(value)
        return lax.psum(value, "dp", axis_index_groups=lines)

    def other_half(value):
        return (value, sums.swap(value, "dp", 1))

    tiles = up_weight.shape[1] // depth
    back = [backward(0, 2)]
    u_terms = sums.halves(then(u_terms))
    d_terms = sums.far(then(d_terms))
    back.append(backward(2, 1))
    u_value = line_sum(then(u_terms), True)
    back.append(backward(3, 1))
    d_terms = sums.halves(then(d_terms))
    a_terms = sums.near(units(back))
    back.append(backward(4, 1))
    a_terms = sums.far(then(a_terms))
    d_value = line_sum(after(d_terms, done, u_value), False)
    done.append(u_value)
    back.append(backward(5, 1))
    a_terms = sums.halves(then(a_terms))
    u_pair = other_half(then(u_value))
    c_terms = sums.near(units(back[3:]))
    c_terms = sums.far(then(c_terms))
    dab = after(dab, sums.sent, done)
    token_grad = token_grad_pass(dab, back, wq, wk, wv)
    done[:] = [token_grad]
    a_terms = sums.pair_up(then(a_terms), rest[0])
    c_terms = sums.pair_up(then(c_terms), 1)
    for bit in rest[1:]:
        a_terms = sums.pair_up(then(a_terms), bit)
    (d_up,) = finish(
        side, [after(u_pair, sums.sent, done)], depth,
        [[((0, t * rows, 0), (rows, depth), (0, t * depth)) for t in range(tiles)]],
    )
    done[:] = [d_up]
    d_pair = other_half(then(d_value))
    for bit in rest:
        c_terms = sums.pair_up(c_terms, bit)
    a_pair = other_half(total(a_terms).astype(BF))

    height = down_weight.shape[0]
    unit = depth // 3
    place = [(0, 0), (0, rows), (1, 0)]
    d_down, d_out, thin = finish(
        side, [d_pair], depth,
        [
            [((0, 0, 0), (height, depth), (0, 0))],
            [((0, height, 0), (rows, depth), (0, 0))],
            [((0, height + rows, 0), (16, depth), (0, 0))],
        ],
    )
    d_q, d_k, d_v, bias = finish(
        side, [a_pair, c_terms], depth,
        [
            [((i, row, t * unit), (rows, unit), (0, u * unit)) for u, (i, row) in enumerate(place)]
            for t in range(3)
        ]
        + [[((0, 2 * rows, 0), (16, depth), (0, 0)), ((1, rows, 0), (16, depth), (16, 0))]],
    )

    def own(z):
        return lax.dynamic_slice_in_dim(z, me_scalar * rows, rows, z.ndim - 1)

    b_o, b_d, gain1, shift1, gain2, shift2 = own(thin[:6])
    b_up = lax.dynamic_slice_in_dim(thin[8 : 8 + tiles].reshape(-1), me_scalar * wide_rows, wide_rows, 0)
    bias = jnp.stack([bias[0], bias[1], bias[16]]).reshape(3, 3, unit).transpose(1, 0, 2)
    b_q, b_k, b_v = own(bias.reshape(3, depth))
    return (
        y, token_grad, d_q, d_k, d_v, d_out, d_up, d_down,
        b_q, b_k, b_v, b_o, b_up, b_d, gain1, shift1, gain2, shift2,
    )


def solution(mesh):
    rows = P(("dp", "fsdp"), None)
    mat = P("fsdp", None)
    vector = P("fsdp")
    in_specs = (rows, rows, P(("dp", "fsdp")), rows) + (mat,) * 6 + (vector,) * 10
    out_specs = (rows, rows) + (mat,) * 6 + (vector,) * 10
    return jax.shard_map(shards, mesh=mesh, in_specs=in_specs, out_specs=out_specs, check_vma=False)
```
